256 devices in a mesh: row: 8 (over y, core), col: 32 (over z, x).
Axes of the slice: x: 4, y: 4, z: 8, core: 2. Of those that a mesh axis runs over, the one named last changes fastest.
Arguments:
- features: bfloat16 [4, 8, 32, 16, 512], P(None, 'row', 'col'), may hold values from -4 to 4, as said below
- left_factor: bfloat16 [4, 8, 512, 2, 32, 512], P(None, 'row', None, None, 'col'), as said below
- ard_weights: float32 [512], replicated, as said below
Outputs:
- panels: float32 [4, 8, 32, 16, 1024], P(None, 'row', 'col')
The draws below stay inside these ranges and needn't reach their ends.
Inputs may be any that keep to these rules, and one draw needn't show every extreme that they name: `features`: independent entries of unit spread. `left_factor`: kernel minus left_update is positive definite on the first 1024 rows. `ard_weights`: independent positive entries between 0.005 and 0.18.
All inputs are finite; a program needn't handle non-finite values.
Results may differ from the reference program's by a relative error of at most 0.0003.
Values may be sent and summed in bfloat16 or wider, within the bound.
A program may use at most 64 MiB of HBM per device.

```python
import math
import jax
import jax.numpy as jnp
from jax import lax

B = 512
F = 512
RB_DEV = 4
LB_DEV = 2
NW = 16384
LEFT = 32768
BS = 16
N_ROW = 8
N_COL = 32


def draw_features(key, part):
    key = jax.random.fold_in(key, 11)
    full_shape = (RB_DEV, N_ROW, N_COL, BS, F)
    values = jnp.clip(jax.random.normal(key, full_shape, jnp.float32), -4.0, 4.0)
    return values.astype(jnp.bfloat16)


def draw_left_factor(key, part):
    key = jax.random.fold_in(key, 23)
    magnitude_key = jax.random.fold_in(key, 1)
    scale_key = jax.random.fold_in(key, 2)
    choose_key = jax.random.fold_in(key, 3)
    rows_all = RB_DEV * N_ROW * B
    cols_all = LB_DEV * N_COL * B
    panel_rows = 2 * B
    uniform_draw = jax.random.uniform(magnitude_key, (rows_all, cols_all), jnp.float32, -1.0, 1.0)
    magnitude = jnp.where(uniform_draw >= 0.0, 0.5 + 0.5 * uniform_draw, -0.5 + 0.5 * uniform_draw)
    block_scale = jnp.exp(0.5 * jax.random.uniform(scale_key, (LB_DEV * N_COL,), jnp.float32, math.log(0.5), math.log(2.0)))
    column_scale = jnp.repeat(block_scale, B)
    basis = magnitude * column_scale[None, :] * math.sqrt(0.08 / LEFT)
    panel_part = basis[:panel_rows]
    chosen_rows = jax.random.randint(choose_key, (rows_all - panel_rows, 4), 0, panel_rows)
    mixed = 0.6 * basis[panel_rows:]
    for choice_idx in range(4):
        mixed = mixed + 0.8 * jnp.take(panel_part, chosen_rows[:, choice_idx], axis=0)
    whole = jnp.concatenate([panel_part, mixed], axis=0)
    return whole.reshape(RB_DEV, N_ROW, B, LB_DEV, N_COL, B).astype(jnp.bfloat16)


def draw_ard_weights(key, part):
    key = jax.random.fold_in(key, 37)
    low_end = math.log(0.005)
    exponent = jax.random.uniform(key, (F,), jnp.float32, low_end, math.log(0.18))
    return jnp.exp(exponent)


def setup_inputs(seed: int = 0) -> dict:
    key_of = jax.random.split(jax.random.key(seed), 4)
    features = draw_features(jax.random.fold_in(key_of[3], 71), 0)
    left_factor = draw_left_factor(jax.random.fold_in(key_of[3], 71), 0)
    ard_weights = draw_ard_weights(jax.random.fold_in(key_of[3], 71), 0)
    return {"features": features, "left_factor": left_factor, "ard_weights": ard_weights}


def contract_rows(left_mat, right_mat):
    return lax.dot_general(left_mat.astype(jnp.float32), right_mat.astype(jnp.float32), (((1,), (1,)), ((), ())), precision=lax.Precision.HIGHEST, preferred_element_type=jnp.float32)

def inverse_factor(matrix):
    factor = jnp.linalg.cholesky(matrix)
    identity_mat = jnp.eye(matrix.shape[0], dtype=jnp.float32)
    return jax.scipy.linalg.solve_triangular(factor, identity_mat, lower=True)

def kernel_block(rows_feat, panel_feat, ard_weights, row_ids, col_ids):
    scaled_rows = rows_feat.astype(jnp.float32) * ard_weights
    scaled_panel = panel_feat.astype(jnp.float32) * ard_weights
    sq_dist = jnp.sum(scaled_rows * scaled_rows, axis=1)[:, None] + jnp.sum(scaled_panel * scaled_panel, axis=1)[None, :] - 2.0 * contract_rows(scaled_rows, scaled_panel)
    jitter = jnp.where(row_ids[:, None] == col_ids[None, :], 0.01, 0.0).astype(jnp.float32)
    return jnp.exp(-0.5 * sq_dist) + jitter

def reference(features, left_factor, ard_weights):
    all_rows = features.reshape(NW, F)
    factor_rows = left_factor.reshape(NW // B, B, LEFT)
    panel_factor = factor_rows[:2].reshape(2 * B, LEFT)

    def block_update(rows_block):
        return lax.dot_general(rows_block.astype(jnp.float32), panel_factor.astype(jnp.float32), (((1,), (1,)), ((), ())), preferred_element_type=jnp.float32)
    left_update = lax.map(block_update, factor_rows).reshape(NW, 2 * B)
    row_ids = jnp.arange(NW, dtype=jnp.int32)
    kernel = kernel_block(all_rows, all_rows[:2 * B], ard_weights, row_ids, row_ids[:2 * B])
    schur = kernel - left_update
    first_inv = inverse_factor(schur[:B, :B])
    first_panel = contract_rows(schur[:, :B], first_inv)
    lower_rows = first_panel[B:2 * B]
    second_schur = schur[:, B:] - contract_rows(first_panel, lower_rows)
    second_inv = inverse_factor(second_schur[B:2 * B])
    second_panel = contract_rows(second_schur, second_inv)
    panels = jnp.concatenate([first_panel, second_panel], axis=1)
    return panels.reshape(RB_DEV, N_ROW, N_COL, BS, 2 * B)
```

```python
import functools

import jax
import jax.numpy as jnp
from jax import lax
from jax.experimental import pallas as pl
from jax.experimental.pallas import tpu as pltpu
from jax.sharding import PartitionSpec as P

HIGHEST = lax.Precision.HIGHEST
MESH = pl.DeviceIdType.MESH
F32 = jnp.float32

NY, NX, NZ = 4, 4, 8
BLOCK = 512
PANELS = 2
SHARE = 16
LANES = 128
SPLITS = BLOCK // LANES
CHUNKS = 8
CHUNK_ROWS = BLOCK // CHUNKS
ROUNDS = ((0, 1), (1, 3))
HOPS = 6


def nt(left, right, precision=HIGHEST):
    return lax.dot_general(
        left, right, (((1,), (1,)), ((), ())), precision=precision, preferred_element_type=F32
    )


def sub_row(tile, j):
    return jnp.broadcast_to(tile[j : j + 1, :], (8, LANES))


def lane_col(tile, j):
    return jnp.broadcast_to(tile[:, j : j + 1], (8, LANES))


def diag_inverse(load_tile, store_tile):
    rows = lax.broadcasted_iota(jnp.int32, (8, LANES), 0)
    lanes = lax.broadcasted_iota(jnp.int32, (8, LANES), 1)
    tiles = LANES // 8
    a = [load_tile(v) for v in range(tiles)]
    e = [jnp.where(lanes == rows + 8 * v, 1.0, 0.0).astype(F32) for v in range(tiles)]
    for g in range(tiles):
        c = [lane_col(a[g], 8 * g + j) for j in range(8)]
        ta, tb, tf = a[g], e[g], e[g]
        scale = jnp.zeros((8, LANES), F32)
        for j in range(8):
            pivot = sub_row(c[j], j)
            recip = 1.0 / pivot
            scale = jnp.where(rows == j, lax.rsqrt(pivot), scale)
            cj = c[j]
            below = jnp.where(rows > j, cj, 0.0)

            def step(tile):
                unit = sub_row(tile, j) * recip
                return jnp.where(rows == j, unit, tile - cj * unit)

            for k in range(j + 1, 8):
                c[k] = step(c[k])
            if g < tiles - 1:
                ta, tb = step(ta), step(tb)
            tf = tf - below * (sub_row(tf, j) * recip)
        store_tile(g, tf * scale)
        if g < tiles - 1:
            wa = [sub_row(ta, j) for j in range(8)]
            wb = [sub_row(tb, j) for j in range(8)]
            for v in range(g + 1, tiles):
                m = [lane_col(a[v], 8 * g + j) for j in range(8)]

                def less(tile, w):
                    p = [m[j] * w[j] for j in range(8)]
                    return tile - (((p[0] + p[1]) + (p[2] + p[3])) + ((p[4] + p[5]) + (p[6] + p[7])))

                a[v] = less(a[v], wa)
                e[v] = less(e[v], wb)


def factor_kernel(s_ref, own_ref, out_ref, a, x, lp):
    n = s_ref.shape[0]
    a[:n, :] = s_ref[...]
    a[n:, :] = own_ref[...]

    def block(b, carry):
        off = pl.multiple_of(b * LANES, LANES)

        def load_tile(v):
            return a[pl.ds(pl.multiple_of(off + 8 * v, 8), 8), pl.ds(off, LANES)]

        def store_tile(g, tile):
            x[8 * g : 8 * g + 8, :] = tile

        diag_inverse(load_tile, store_tile)
        lp[...] = nt(a[:, pl.ds(off, LANES)], x[...])
        out_ref[:, pl.ds(off, LANES)] = lp[n:, :]

        def col(c, carry):
            coff = pl.multiple_of(c * LANES, LANES)
            a[:, pl.ds(coff, LANES)] -= nt(lp[...], lp[pl.ds(coff, LANES), :])
            return carry

        lax.fori_loop(b + 1, n // LANES, col, 0)
        return carry

    lax.fori_loop(0, n // LANES, block, 0)


def factor_panels(s_all, s_own):
    n, own = s_all.shape[0], s_own.shape[0]
    vmem = pl.BlockSpec(memory_space=pltpu.VMEM)
    return pl.pallas_call(
        factor_kernel,
        out_shape=jax.ShapeDtypeStruct((own, n), F32),
        in_specs=[vmem, vmem],
        out_specs=vmem,
        scratch_shapes=[
            pltpu.VMEM((n + own, n), F32),
            pltpu.VMEM((LANES, LANES), F32),
            pltpu.VMEM((n + own, LANES), F32),
        ],
        compiler_params=pltpu.CompilerParams(vmem_limit_bytes=48 * 2**20),
    )(s_all, s_own)


def ring_add(m, k, n):
    return lax.rem(m + (k + n), n)


def comm_kernel(
    lf, feats, wts, s_all, s_own,
    pan, fp, t, kern, bz1, bx1, bx2, bz2, sa, so,
    pan_s, pan_r, ft_s, ft_r, rs_s, rs_r, ag_s, ag_r, loc,
):
    row, col = lax.axis_index("row"), lax.axis_index("col")
    y, core = row // 2, lax.rem(row, 2)
    mz, mx = col // NX, lax.rem(col, NX)
    at_y0 = y == 0

    def dev(dy=0, dx=0, dz=0, other=False):
        yy, xx, zz = ring_add(y, dy, NY), ring_add(mx, dx, NX), ring_add(mz, dz, NZ)
        cc = 1 - core if other else core
        return (yy * 2 + cc, zz * NX + xx)

    yp, ym = dev(dy=1), dev(dy=-1)
    zp, zm = dev(dz=1), dev(dz=-1)
    xp, xm = dev(dx=1), dev(dx=-1)
    sib = dev(other=True)

    def rcopy(src, dst, ssem, rsem, target):
        return pltpu.make_async_remote_copy(
            src_ref=src, dst_ref=dst, send_sem=ssem, recv_sem=rsem,
            device_id=target, device_id_type=MESH,
        )

    barrier = pltpu.get_barrier_semaphore()
    for target in (yp, ym, zp, zm, xp, xm, sib):
        pl.semaphore_signal(barrier, inc=1, device_id=target, device_id_type=MESH)
    pl.semaphore_wait(barrier, 7)

    def gather_ops(n, m, slot, ssem, rsem, plus, minus, arrived=None):
        hp, hm = n // 2, n // 2 - 1

        def up(s):
            ref = slot(ring_add(m, -s, n))
            return rcopy(ref, ref, ssem(s), rsem(s), plus)

        def down(s):
            ref = slot(ring_add(m, s, n))
            return rcopy(ref, ref, ssem(hp + s), rsem(hp + s), minus)

        def start():
            up(0).start()
            down(0).start()
            if arrived is not None:
                arrived(m, 0)

        def step(s):
            k = ring_add(m, -1 - s, n)
            rcopy(slot(k), slot(k), ssem(s), rsem(s), plus).wait_recv()
            if s < hp - 1:
                up(s + 1).start()
            if arrived is not None:
                arrived(k, 1 + s)
            if s < hm:
                k = ring_add(m, 1 + s, n)
                rcopy(slot(k), slot(k), ssem(hp + s), rsem(hp + s), minus).wait_recv()
                if s < hm - 1:
                    down(s + 1).start()
                if arrived is not None:
                    arrived(k, 1 + hp + s)

        def drain():
            for s in range(hp):
                up(s).wait_send()
            for s in range(hm):
                down(s).wait_send()

        return start, step, drain

    def spread_ops(ref, ssem0, ssem1, rsem):
        def go():
            @pl.when(at_y0)
            def _():
                rcopy(ref, ref, ssem0, rsem, yp).start()
                rcopy(ref, ref, ssem1, rsem, ym).start()

            @pl.when(jnp.logical_not(at_y0))
            def _():
                rcopy(ref, ref, ssem0, rsem, yp).wait_recv()

            @pl.when(y == 1)
            def _():
                rcopy(ref, ref, ssem0, rsem, yp).start()

        def drain():
            @pl.when(y <= 1)
            def _():
                rcopy(ref, ref, ssem0, rsem, yp).wait_send()

            @pl.when(at_y0)
            def _():
                rcopy(ref, ref, ssem1, rsem, ym).wait_send()

        return go, drain

    pos = jnp.where(core == 0, y, ring_add(0, NY - y, NY))
    onward = (jnp.where(core == 0, yp[0], ym[0]), col)

    def pan_ref(b, c):
        return pan.at[b, pl.ds(c * CHUNK_ROWS, CHUNK_ROWS)]

    def ring_chunk(c):
        return rcopy(pan_ref(core, c), pan_ref(core, c), pan_s.at[0, c], pan_r.at[0, c], onward)

    def sib_chunk(c, b):
        return rcopy(pan_ref(b, c), pan_ref(b, c), pan_s.at[1, c], pan_r.at[1, c], sib)

    @pl.when(at_y0)
    def _():
        fp[core, mz, mx] = feats[0]
        own = pltpu.make_async_copy(lf.at[0], pan.at[core], loc.at[0])
        own.start()
        own.wait()

    f_spread, f_spread_drain = spread_ops(fp.at[core, mz, mx], ft_s.at[0], ft_s.at[1], ft_r.at[0])
    fx = gather_ops(NX, mx, lambda k: fp.at[core, mz, k], lambda i: ft_s.at[2 + i], lambda i: ft_r.at[2 + i], xp, xm)
    fz = gather_ops(NZ, mz, lambda k: fp.at[core, k], lambda i: ft_s.at[5 + i], lambda i: ft_r.at[5 + i], zp, zm)

    def f_sib(b):
        return rcopy(fp.at[b], fp.at[b], ft_s.at[12], ft_r.at[12], sib)

    def f_step(i):
        if i == 0:
            f_spread()
            fx[0]()
        elif i == 1:
            fx[1](0)
        elif i == 2:
            fx[1](1)
            fz[0]()
        elif i < 7:
            fz[1](i - 3)
        else:
            f_sib(core).start()

    def stream(b, h, rnd):
        i0, ni = ROUNDS[rnd]
        isl = pl.ds(i0, ni)
        q = b * SPLITS + h
        w = h // 2
        z_first = h % 2 == 0

        def part(axis, k):
            if z_first:
                return t.at[q, k, isl] if axis == "z" else t.at[q, mz, isl, k]
            return t.at[q, :, isl, k] if axis == "x" else t.at[q, k, isl, mx]

        def slot(axis, s):
            if z_first:
                return bz1.at[b, w, s, isl] if axis == "z" else bx2.at[b, w, s, isl]
            return bx1.at[b, w, s, :, isl] if axis == "x" else bz2.at[b, w, s, isl]

        order = ("z", "x") if z_first else ("x", "z")
        size = {"z": (NZ, mz, zp, zm), "x": (NX, mx, xp, xm)}
        base = {order[0]: 0, order[1]: size[order[0]][0] - 1}

        def copy(axis, src, s, target):
            i = base[axis] + s
            return rcopy(src, slot(axis, s), rs_s.at[rnd, q, i], rs_r.at[rnd, q, i], target)

        def begin(axis):
            n, m, plus, minus = size[axis]
            hp, hm = n // 2, n // 2 - 1
            copy(axis, part(axis, ring_add(m, hp, n)), 0, plus).start()
            copy(axis, part(axis, ring_add(m, -hm, n)), hp, minus).start()

        def hop(axis, s):
            n, m, plus, minus = size[axis]
            hp, hm = n // 2, n // 2 - 1
            here = slot(axis, s)
            copy(axis, here, s, plus).wait_recv()
            if s < hp - 1:
                here[...] = here[...] + part(axis, ring_add(m, hp - 1 - s, n))[...]
                copy(axis, here, s + 1, plus).start()
            if s < hm:
                there = slot(axis, hp + s)
                copy(axis, there, hp + s, minus).wait_recv()
                if s < hm - 1:
                    there[...] = there[...] + part(axis, ring_add(m, s + 1 - hm, n))[...]
                    copy(axis, there, hp + s + 1, minus).start()
            if s == hp - 1:
                mine = part(axis, m)
                mine[...] = mine[...] + (here[...] + slot(axis, hp + hm - 1)[...])
                if axis == order[0]:
                    begin(order[1])

        def macro(g):
            first = size[order[0]][0] // 2
            if g < first:
                hop(order[0], g)
            else:
                hop(order[1], g - first)

        def drain():
            for axis in order:
                n, m, plus, minus = size[axis]
                for s in range(n - 1):
                    copy(axis, slot(axis, s), s, plus).wait_send()

        return (lambda: begin(order[0])), macro, drain

    def rs_hop(rnd, g):
        for h in range(SPLITS):
            for b in range(PANELS):
                stream(b, h, rnd)[1](g)

    def product(b, h, i):
        rows = nt(lf[i], pan[b, h * LANES : (h + 1) * LANES, :], None)
        t[b * SPLITS + h, :, i] = rows.reshape(NZ, NX, SHARE, LANES)

    for c in range(CHUNKS):
        @pl.when(jnp.logical_not(at_y0))
        def _():
            ring_chunk(c).wait_recv()

        @pl.when(pos < NY - 1)
        def _():
            ring_chunk(c).start()

        sib_chunk(c, core).start()
        f_step(c)
        sib_chunk(c, 1 - core).wait_recv()
        if c % 2 == 1:
            for b in (core, 1 - core):
                product(b, c // 2, 0)
                stream(b, c // 2, 0)[0]()

    f_sib(1 - core).wait_recv()
    weights = wts[...]
    own_feat = feats[...].reshape(4 * SHARE, -1).astype(F32) * weights
    own_norm = jnp.sum(own_feat * own_feat, axis=1, keepdims=True)
    ids = lax.broadcasted_iota(jnp.int32, (4 * SHARE, BLOCK), 0)
    row_ids = ((ids // SHARE) * 8 + row) * BLOCK + col * SHARE + lax.rem(ids, SHARE)
    for b in range(PANELS):
        feat = fp[b].reshape(BLOCK, -1).astype(F32) * weights
        norm = nt(jnp.ones((8, feat.shape[1]), F32), feat * feat)[0:1, :]
        dist = own_norm + norm - 2.0 * nt(own_feat, feat)
        cols = lax.broadcasted_iota(jnp.int32, (4 * SHARE, BLOCK), 1) + b * BLOCK
        kern[:, b * BLOCK : (b + 1) * BLOCK] = jnp.exp(-0.5 * dist) + jnp.where(row_ids == cols, 0.01, 0.0).astype(F32)

    def rest(i, carry):
        for b in range(PANELS):
            for h in range(SPLITS):
                product(b, h, i)
        return carry

    lax.fori_loop(1, 4, rest, 0)

    rs_hop(0, 0)
    rs_hop(0, 1)
    for h in range(SPLITS):
        for b in range(PANELS):
            stream(b, h, 1)[0]()
    for g in range(2, HOPS):
        rs_hop(0, g)

    def schur(i):
        for q in range(PANELS * SPLITS):
            lanes = pl.ds(q * LANES, LANES)
            so[i, :, lanes] = kern[i * SHARE : (i + 1) * SHARE, lanes] - t[q, mz, i, mx]

    schur(0)

    left, right = pl.ds(0, BLOCK), pl.ds(BLOCK, BLOCK)
    sa[0, :, :, :, right] = jnp.zeros((NZ, NX, SHARE, BLOCK), F32)

    @pl.when(at_y0)
    def _():
        sa[core, mz, mx, :, left] = so[0, :, left]

        @pl.when(core == 1)
        def _():
            sa[1, mz, mx, :, right] = so[0, :, right]

    def to_sib(half, b, k, i):
        ref = sa.at[b, k, :, :, left] if half == 0 else sa.at[b, :, k, :, right]
        return rcopy(ref, ref, ag_s.at[half, 12 + i], ag_r.at[half, 12 + i], sib)

    def ag_sems(sems, half, base):
        return lambda i: sems.at[half, base + i]

    g0_spread, g0_spread_drain = spread_ops(sa.at[core, mz, mx, :, left], ag_s.at[0, 0], ag_s.at[0, 1], ag_r.at[0, 0])
    g0x = gather_ops(NX, mx, lambda k: sa.at[core, mz, k, :, left], ag_sems(ag_s, 0, 2), ag_sems(ag_r, 0, 2), xp, xm)
    g0z = gather_ops(NZ, mz, lambda k: sa.at[core, k, :, :, left], ag_sems(ag_s, 0, 5), ag_sems(ag_r, 0, 5), zp, zm,
                     lambda k, i: to_sib(0, core, k, i).start())
    g1_spread, g1_spread_drain = spread_ops(sa.at[1, mz, mx, :, right], ag_s.at[1, 0], ag_s.at[1, 1], ag_r.at[1, 0])
    g1z = gather_ops(NZ, mz, lambda k: sa.at[1, k, mx, :, right], ag_sems(ag_s, 1, 2), ag_sems(ag_r, 1, 2), zp, zm)
    g1x = gather_ops(NX, mx, lambda k: sa.at[1, :, k, :, right], ag_sems(ag_s, 1, 9), ag_sems(ag_r, 1, 9), xp, xm,
                     lambda k, i: to_sib(1, 1, k, i).start())

    def on_core1(fn):
        pl.when(core == 1)(fn)

    g0_spread()
    on_core1(g1_spread)
    g0x[0]()
    on_core1(g1z[0])
    g0x[1](0)
    g0x[1](1)
    g0z[0]()
    on_core1(lambda: g1z[1](0))
    on_core1(lambda: g1z[1](1))
    rs_hop(1, 0)
    g0z[1](0)
    g0z[1](1)

    def g1_mid():
        g1z[1](2)
        g1z[1](3)
        g1x[0]()

    on_core1(g1_mid)
    g0z[1](2)
    g0z[1](3)

    def g1_end():
        g1x[1](0)
        g1x[1](1)

    on_core1(g1_end)
    for i in range(NZ):
        k = ring_add(mz, (0, -1, -2, -3, -4, 1, 2, 3)[i], NZ)
        to_sib(0, 1 - core, k, i).wait_recv()

    @pl.when(core == 0)
    def _():
        for i in range(NX):
            k = ring_add(mx, (0, -1, -2, 1)[i], NX)
            to_sib(1, 1, k, i).wait_recv()

    for g in range(1, HOPS):
        rs_hop(1, g)
    for i in range(1, 4):
        schur(i)

    out_all = pltpu.make_async_copy(sa, s_all, loc.at[1])
    out_own = pltpu.make_async_copy(so, s_own, loc.at[2])
    out_all.start()
    out_own.start()

    @pl.when(pos < NY - 1)
    def _():
        for c in range(CHUNKS):
            ring_chunk(c).wait_send()

    for c in range(CHUNKS):
        sib_chunk(c, core).wait_send()
    f_spread_drain()
    fx[2]()
    fz[2]()
    f_sib(core).wait_send()
    for rnd in range(2):
        for b in range(PANELS):
            for h in range(SPLITS):
                stream(b, h, rnd)[2]()
    g0_spread_drain()
    g0x[2]()
    g0z[2]()
    for i in range(NZ):
        to_sib(0, core, 0, i).wait_send()

    def g1_drain():
        g1_spread_drain()
        g1z[2]()
        g1x[2]()
        for i in range(NX):
            to_sib(1, 1, 0, i).wait_send()

    on_core1(g1_drain)
    out_all.wait()
    out_own.wait()


def schur_rows(lf, feats, wts):
    vmem = pl.BlockSpec(memory_space=pltpu.VMEM)
    anyspace = pl.BlockSpec(memory_space=pl.ANY)
    width = lf.shape[2]
    fwidth = feats.shape[2]
    dma = pltpu.SemaphoreType.DMA
    return pl.pallas_call(
        comm_kernel,
        out_shape=(
            jax.ShapeDtypeStruct((PANELS, NZ, NX, SHARE, PANELS * BLOCK), F32),
            jax.ShapeDtypeStruct((4, SHARE, PANELS * BLOCK), F32),
        ),
        in_specs=[vmem, vmem, vmem],
        out_specs=(anyspace, anyspace),
        scratch_shapes=[
            pltpu.VMEM((PANELS, BLOCK, width), jnp.bfloat16),
            pltpu.VMEM((PANELS, NZ, NX, SHARE, fwidth), jnp.bfloat16),
            pltpu.VMEM((PANELS * SPLITS, NZ, 4, NX, SHARE, LANES), F32),
            pltpu.VMEM((4 * SHARE, PANELS * BLOCK), F32),
            pltpu.VMEM((PANELS, 2, NZ - 1, 4, NX, SHARE, LANES), F32),
            pltpu.VMEM((PANELS, 2, NX - 1, NZ, 4, SHARE, LANES), F32),
            pltpu.VMEM((PANELS, 2, NX - 1, 4, SHARE, LANES), F32),
            pltpu.VMEM((PANELS, 2, NZ - 1, 4, SHARE, LANES), F32),
            pltpu.VMEM((PANELS, NZ, NX, SHARE, PANELS * BLOCK), F32),
            pltpu.VMEM((4, SHARE, PANELS * BLOCK), F32),
            dma((2, CHUNKS)), dma((2, CHUNKS)),
            dma((13,)), dma((13,)),
            dma((2, PANELS * SPLITS, 10)), dma((2, PANELS * SPLITS, 10)),
            dma((2, 20)), dma((2, 20)),
            dma((3,)),
        ],
        compiler_params=pltpu.CompilerParams(
            collective_id=0, has_side_effects=True, vmem_limit_bytes=56 * 2**20
        ),
    )(lf, feats, wts)


def per_device(features, left_factor, ard_weights):
    lf = left_factor.reshape(4, BLOCK, -1)
    feats = features.reshape(4, SHARE, -1)
    s_all, s_own = schur_rows(lf, feats, ard_weights.reshape(1, -1))
    panels = factor_panels(s_all.reshape(PANELS * BLOCK, -1), s_own.reshape(4 * SHARE, -1))
    return panels.reshape(4, 1, 1, SHARE, PANELS * BLOCK)


def solution(mesh):
    return jax.shard_map(
        per_device,
        mesh=mesh,
        in_specs=(P(None, "row", "col", None, None), P(None, "row", None, None, "col", None), P()),
        out_specs=P(None, "row", "col", None, None),
        check_vma=False,
    )
```

```python
import functools

import jax
import jax.numpy as jnp
from jax import lax
from jax.experimental import pallas as pl
from jax.experimental.pallas import tpu as pltpu
from jax.sharding import PartitionSpec as P

HIGHEST = lax.Precision.HIGHEST
MESH = pl.DeviceIdType.MESH
F32 = jnp.float32

NY, NX, NZ = 4, 4, 8
BLOCK = 512
PANELS = 2
SHARE = 16
LANES = 128
SPLITS = BLOCK // LANES
CHUNKS = 8
CHUNK_ROWS = BLOCK // CHUNKS
ROUNDS = ((0, 4), (1, 3))
HOPS = 6
BF16 = jnp.bfloat16


def nt(left, right, precision=HIGHEST):
    return lax.dot_general(
        left, right, (((1,), (1,)), ((), ())), precision=precision, preferred_element_type=F32
    )


def sub_row(tile, j):
    return jnp.broadcast_to(tile[j : j + 1, :], (8, LANES))


def lane_col(tile, j):
    return jnp.broadcast_to(tile[:, j : j + 1], (8, LANES))


def diag_inverse(load_tile, store_tile):
    rows = lax.broadcasted_iota(jnp.int32, (8, LANES), 0)
    lanes = lax.broadcasted_iota(jnp.int32, (8, LANES), 1)
    tiles = LANES // 8
    a = [load_tile(v) for v in range(tiles)]
    e = [jnp.where(lanes == rows + 8 * v, 1.0, 0.0).astype(F32) for v in range(tiles)]
    for g in range(tiles):
        c = [lane_col(a[g], 8 * g + j) for j in range(8)]
        ta, tb, tf = a[g], e[g], e[g]
        scale = jnp.zeros((8, LANES), F32)
        for j in range(8):
            pivot = sub_row(c[j], j)
            recip = 1.0 / pivot
            scale = jnp.where(rows == j, lax.rsqrt(pivot), scale)
            cj = c[j]
            below = jnp.where(rows > j, cj, 0.0)

            def step(tile):
                unit = sub_row(tile, j) * recip
                return jnp.where(rows == j, unit, tile - cj * unit)

            for k in range(j + 1, 8):
                c[k] = step(c[k])
            if g < tiles - 1:
                ta, tb = step(ta), step(tb)
            tf = tf - below * (sub_row(tf, j) * recip)
        store_tile(g, tf * scale)
        if g < tiles - 1:
            wa = [sub_row(ta, j) for j in range(8)]
            wb = [sub_row(tb, j) for j in range(8)]
            for v in range(g + 1, tiles):
                m = [lane_col(a[v], 8 * g + j) for j in range(8)]

                def less(tile, w):
                    p = [m[j] * w[j] for j in range(8)]
                    return tile - (((p[0] + p[1]) + (p[2] + p[3])) + ((p[4] + p[5]) + (p[6] + p[7])))

                a[v] = less(a[v], wa)
                e[v] = less(e[v], wb)


def halves(value):
    high = value.astype(BF16)
    return high, (value - high.astype(F32)).astype(BF16)


def nt_halves(left, right):
    return nt(left[0], right[0], None) + (nt(left[0], right[1], None) + nt(left[1], right[0], None))


def ring_add(m, k, n):
    return lax.rem(m + (k + n), n)


def panels_kernel(
    lf_in, feats, wts, out_ref,
    raw, rt, lf, pan, fp, t, kern, bz1, bx1, bx2, bz2, rx, rz, sa, own_s,
    lo, xs, col_buf, dg, po,
    pan_s, pan_r, ft_s, ft_r, rs_s, rs_r, dg_s, dg_r, loc,
):
    row, col = lax.axis_index("row"), lax.axis_index("col")
    y, core = row // 2, lax.rem(row, 2)
    mz, mx = col // NX, lax.rem(col, NX)
    at_y0 = y == 0
    off_y0 = jnp.logical_not(at_y0)
    n_cols = PANELS * BLOCK

    def dev(dy=0, dx=0, dz=0, other=False):
        yy, xx, zz = ring_add(y, dy, NY), ring_add(mx, dx, NX), ring_add(mz, dz, NZ)
        cc = 1 - core if other else core
        return (yy * 2 + cc, zz * NX + xx)

    yp, ym = dev(dy=1), dev(dy=-1)
    zp, zm = dev(dz=1), dev(dz=-1)
    xp, xm = dev(dx=1), dev(dx=-1)
    sib = dev(other=True)

    def rcopy(src, dst, ssem, rsem, target):
        return pltpu.make_async_remote_copy(
            src_ref=src, dst_ref=dst, send_sem=ssem, recv_sem=rsem,
            device_id=target, device_id_type=MESH,
        )

    raw_copies = [pltpu.make_async_copy(lf_in.at[i], raw.at[i], loc.at[i]) for i in range(4)]
    for copy in raw_copies:
        copy.start()
    barrier = pltpu.get_barrier_semaphore()
    peers = [dev(dz=k) for k in range(1, NZ)] + [dev(dx=k) for k in range(1, NX)]
    peers += [dev(dy=k) for k in range(1, NY)] + [sib]
    for target in peers:
        pl.semaphore_signal(barrier, inc=1, device_id=target, device_id_type=MESH)

    def relayout(i, c, stores):
        rows = pl.ds(c * CHUNK_ROWS, CHUNK_ROWS)
        value = raw[i, rows].astype(F32).reshape(2 * CHUNK_ROWS, BLOCK)
        for lane in range(SPLITS):
            rt[lane] = value[:, lane * LANES : (lane + 1) * LANES]
        for j in range(2):
            for lane in range(SPLITS):
                part = rt[lane, pl.ds(j, CHUNK_ROWS, stride=2), :].astype(BF16)
                lanes = pl.ds(j * BLOCK + lane * LANES, LANES)
                for store in stores:
                    store(rows, lanes, part)

    def to_lf(i):
        def store(rows, lanes, part):
            lf[i, rows, lanes] = part

        return store

    def to_pan(rows, lanes, part):
        pan[core, rows, lanes] = part

    def relayout_blocks(first):
        def go(k, carry):
            i, c = first + k // CHUNKS, lax.rem(k, CHUNKS)
            relayout(i, c, [to_lf(i)])
            return carry

        lax.fori_loop(0, (4 - first) * CHUNKS, go, 0)

    pos = jnp.where(core == 0, y, ring_add(0, NY - y, NY))
    onward = (jnp.where(core == 0, yp[0], ym[0]), col)

    def pan_ref(b, c):
        return pan.at[b, pl.ds(c * CHUNK_ROWS, CHUNK_ROWS)]

    def ring_chunk(c):
        return rcopy(pan_ref(core, c), pan_ref(core, c), pan_s.at[0, c], pan_r.at[0, c], onward)

    def sib_chunk(c, b):
        return rcopy(pan_ref(b, c), pan_ref(b, c), pan_s.at[1, c], pan_r.at[1, c], sib)

    def f_slab():
        return fp.at[core, mz, mx]

    def f_y(k):
        return rcopy(f_slab(), f_slab(), ft_s.at[k - 1], ft_r.at[0], dev(dy=k))

    def f_z(k, z):
        ref = fp.at[core, z, mx]
        return rcopy(ref, ref, ft_s.at[2 + k], ft_r.at[2 + k], dev(dz=k))

    def f_x(k, x):
        ref = fp.at[core, :, x]
        return rcopy(ref, ref, ft_s.at[9 + k], ft_r.at[9 + k], dev(dx=k))

    def f_sib(b):
        return rcopy(fp.at[b], fp.at[b], ft_s.at[13], ft_r.at[13], sib)

    def f_z_start():
        for k in range(1, NZ):
            f_z(k, mz).start()

    def f_x_start():
        for k in range(1, NZ):
            f_z(k, ring_add(mz, -k, NZ)).wait_recv()
        for k in range(1, NX):
            f_x(k, mx).start()

    def f_sib_start():
        for k in range(1, NX):
            f_x(k, ring_add(mx, -k, NX)).wait_recv()
        f_sib(core).start()

    def stream(b, h, rnd):
        i0, ni = ROUNDS[rnd]
        isl = pl.ds(i0, ni)
        q = b * SPLITS + h
        w = h // 2
        z_first = h % 2 == 0
        sign = 1 if w == 0 else -1

        def part(axis, k):
            if z_first:
                return t.at[q, k, isl] if axis == "z" else t.at[q, mz, isl, k]
            return t.at[q, :, isl, k] if axis == "x" else t.at[q, k, isl, mx]

        def slot(axis, s):
            if z_first:
                return bz1.at[b, w, s, isl] if axis == "z" else bx2.at[b, w, s, isl]
            return bx1.at[b, w, s, :, isl] if axis == "x" else bz2.at[b, w, s, isl]

        order = ("z", "x") if z_first else ("x", "z")
        size = {
            "z": (NZ, mz) + ((zp, zm) if sign > 0 else (zm, zp)),
            "x": (NX, mx) + ((xp, xm) if sign > 0 else (xm, xp)),
        }
        base = {order[0]: 0, order[1]: size[order[0]][0] - 1}

        def copy(axis, src, s, target):
            i = base[axis] + s
            return rcopy(src, slot(axis, s), rs_s.at[q, i], rs_r.at[q, i], target)

        def begin(axis):
            n, m, plus, minus = size[axis]
            hp, hm = n // 2, n // 2 - 1
            copy(axis, part(axis, ring_add(m, sign * hp, n)), 0, plus).start()
            copy(axis, part(axis, ring_add(m, -sign * hm, n)), hp, minus).start()

        def hop(axis, s):
            n, m, plus, minus = size[axis]
            hp, hm = n // 2, n // 2 - 1
            here = slot(axis, s)
            copy(axis, here, s, plus).wait_recv()
            if s < hp - 1:
                here[...] = here[...] + part(axis, ring_add(m, sign * (hp - 1 - s), n))[...]
                copy(axis, here, s + 1, plus).start()
            if s < hm:
                there = slot(axis, hp + s)
                copy(axis, there, hp + s, minus).wait_recv()
                if s < hm - 1:
                    there[...] = there[...] + part(axis, ring_add(m, sign * (s + 1 - hm), n))[...]
                    copy(axis, there, hp + s + 1, minus).start()
            if s == hp - 1:
                mine = part(axis, m)
                mine[...] = mine[...] + (here[...] + slot(axis, hp + hm - 1)[...])
                if axis == order[0]:
                    begin(order[1])

        def macro(g):
            first = size[order[0]][0] // 2
            if g < first:
                hop(order[0], g)
            else:
                hop(order[1], g - first)

        def drain():
            for axis in order:
                n, m, plus, minus = size[axis]
                for s in range(n - 1):
                    copy(axis, slot(axis, s), s, plus).wait_send()

        return (lambda: begin(order[0])), macro, drain

    def rs_hop(g):
        def go(rnd):
            for h in range(SPLITS):
                for b in range(PANELS):
                    stream(b, h, rnd)[1](g)

        pl.when(off_y0)(lambda: go(0))
        pl.when(at_y0)(lambda: go(1))

    def product(b, h, i):
        rows = nt(lf[i], pan[b, h * LANES : (h + 1) * LANES, :], None)
        t[b * SPLITS + h, :, i] = rows.reshape(NZ, NX, SHARE, LANES)

    def lanes_of(j):
        return pl.ds(j * LANES, LANES)

    def dcopy(src, dst, j, i, target):
        return rcopy(src, dst, dg_s.at[j, i], dg_r.at[j, i], target)

    def rsx(j, k):
        return dcopy(t.at[j, :, 0, ring_add(mx, k, NX)], rx.at[j, k - 1], j, k - 1, dev(dx=k))

    def rsz(j, k):
        return dcopy(t.at[j, ring_add(mz, k, NZ), 0, mx], rz.at[j, k - 1], j, 2 + k, dev(dz=k))

    def agy(j, k):
        ref = sa.at[core, mz, mx, :, lanes_of(j)]
        return rcopy(ref, ref, dg_s.at[j, 9 + k], dg_r.at[j, 10], dev(dy=k))

    def agz(j, k, z):
        ref = sa.at[core, z, mx, :, lanes_of(j)]
        return dcopy(ref, ref, j, 12 + k, dev(dz=k))

    def agx(j, k, x):
        ref = sa.at[core, :, x, :, lanes_of(j)]
        return dcopy(ref, ref, j, 19 + k, dev(dx=k))

    def ags(j, k, b):
        ref = sa.at[b, :, ring_add(mx, -k, NX), :, lanes_of(j)]
        return dcopy(ref, ref, j, 23 + k, sib)

    def gathers(j, fn):
        if j < SPLITS:
            fn()
        else:
            pl.when(core == 1)(fn)

    def rsx_start(j):
        for k in range(1, NX):
            rsx(j, k).start()

    def rsx_done(j):
        for k in range(1, NX):
            rsx(j, k).wait_recv()
        total = t[j, :, 0, mx] + rx[j, 0]
        t[j, :, 0, mx] = total + (rx[j, 1] + rx[j, 2])
        for k in range(1, NZ):
            rsz(j, k).start()

    def rsz_done(j):
        for k in range(1, NZ):
            rsz(j, k).wait_recv()
        total = t[j, mz, 0, mx] + rz[j, 0]
        for k in range(1, NZ - 1, 2):
            total = total + (rz[j, k] + rz[j, k + 1])
        lanes = lanes_of(j)
        schur = kern[0:SHARE, lanes] - total
        own_s[0:SHARE, lanes] = schur

        def send():
            sa[core, mz, mx, :, lanes] = schur
            for k in range(1, NY):
                agy(j, k).start()
            for k in range(1, NZ):
                agz(j, k, mz).start()

        gathers(j, send)

    def agy_done(j):
        def go():
            agy(j, 1).wait_recv()
            for k in range(1, NZ):
                agz(j, k, mz).start()

        gathers(j, go)

    def agz_done(j):
        def go():
            for k in range(1, NZ):
                agz(j, k, ring_add(mz, -k, NZ)).wait_recv()
            for k in range(1, NX):
                agx(j, k, mx).start()
            ags(j, 0, core).start()

        gathers(j, go)

    def agx_done(j):
        def go():
            for k in range(1, NX):
                agx(j, k, ring_add(mx, -k, NX)).wait_recv()
                ags(j, k, core).start()

        gathers(j, go)

    def sib_done(j):
        def go():
            for k in range(NX):
                ags(j, k, 1 - core).wait_recv()

        if j < SPLITS:
            go()
        else:
            pl.when(core == 0)(go)

    def own_kernel():
        weights = wts[...]
        own_feat = feats[...].reshape(4 * SHARE, -1).astype(F32) * weights
        own_norm = jnp.sum(own_feat * own_feat, axis=1, keepdims=True)
        ids = lax.broadcasted_iota(jnp.int32, (4 * SHARE, BLOCK), 0)
        row_ids = ((ids // SHARE) * 8 + row) * BLOCK + col * SHARE + lax.rem(ids, SHARE)
        for b in range(PANELS):
            feat = fp[b].reshape(BLOCK, -1).astype(F32) * weights
            norm = nt(jnp.ones((8, feat.shape[1]), F32), feat * feat)[0:1, :]
            dist = own_norm + norm - 2.0 * nt(own_feat, feat)
            cols = lax.broadcasted_iota(jnp.int32, (4 * SHARE, BLOCK), 1) + b * BLOCK
            jitter = jnp.where(row_ids == cols, 0.01, 0.0).astype(F32)
            kern[:, b * BLOCK : (b + 1) * BLOCK] = jnp.exp(-0.5 * dist) + jitter

    @pl.when(at_y0)
    def _():
        fp[core, mz, mx] = feats[0]

    raw_copies[0].wait()
    pl.semaphore_wait(barrier, len(peers))

    @pl.when(at_y0)
    def _():
        for k in range(1, NY):
            f_y(k).start()
        f_z_start()
        for c in range(CHUNKS):
            relayout(0, c, [to_lf(0), to_pan])
            sib_chunk(c, core).start()
            ring_chunk(c).start()

    lo[...] = jnp.zeros(lo.shape, BF16)
    po[...] = jnp.zeros(po.shape, BF16)
    sa[0, :, :, :, pl.ds(BLOCK, BLOCK)] = jnp.zeros((NZ, NX, SHARE, BLOCK), F32)
    for copy in raw_copies[1:]:
        copy.wait()

    @pl.when(at_y0)
    def _():
        for h in range(SPLITS):
            sib_chunk(2 * h, 1 - core).wait_recv()
            sib_chunk(2 * h + 1, 1 - core).wait_recv()
            product(0, h, 0)
            rsx_start(h)
        f_x_start()
        relayout_blocks(1)

        def rest(b):
            def go(i, carry):
                for h in range(SPLITS):
                    product(b, h, i)
                return carry

            lax.fori_loop(1, 4, go, 0)
            for h in range(SPLITS):
                stream(b, h, 1)[0]()

        rest(0)
        for j in range(SPLITS):
            rsx_done(j)
        f_sib_start()
        for h in range(SPLITS):
            product(1, h, 0)
            rsx_start(SPLITS + h)
        f_sib(1 - core).wait_recv()
        own_kernel()
        for j in range(SPLITS):
            rsz_done(j)
        rest(1)
        for j in range(SPLITS, 2 * SPLITS):
            rsx_done(j)

    @pl.when(off_y0)
    def _():
        relayout_blocks(0)
        f_y(1).wait_recv()
        f_z_start()
        for c in range(CHUNKS):
            ring_chunk(c).wait_recv()

            @pl.when(pos < NY - 1)
            def _():
                ring_chunk(c).start()

            sib_chunk(c, core).start()
            sib_chunk(c, 1 - core).wait_recv()
            if c == 3:
                f_x_start()
            if c % 2 == 1:
                def go(i, carry):
                    product(0, c // 2, i)
                    product(1, c // 2, i)
                    return carry

                lax.fori_loop(0, 4, go, 0)
                for b in range(PANELS):
                    stream(b, c // 2, 0)[0]()
        f_sib_start()
        f_sib(1 - core).wait_recv()
        own_kernel()
        for j in range(SPLITS):
            agy_done(j)

    def store_inverse(b):
        def store(g, tile):
            xs[b, 8 * g : 8 * g + 8, :] = tile

        return store

    def block_of(value):
        return lambda v: value[8 * v : 8 * v + 8, :]

    def rest_of(b):
        off = pl.multiple_of(b * LANES, LANES)
        noff = pl.multiple_of(off + LANES, LANES)
        for i, half in enumerate(halves(nt(col_buf[lax.rem(b, 2)], xs[b]))):
            lo[i, :, pl.ds(off, LANES)] = half
        update = nt_halves((lo[0], lo[1]), (lo[0, pl.ds(noff, LANES), :], lo[1, pl.ds(noff, LANES), :]))
        col_buf[lax.rem(b + 1, 2)] = sa[:, :, :, :, pl.ds(noff, LANES)].reshape(n_cols, LANES) - update

    def next_diag(b):
        off = pl.multiple_of(b * LANES, LANES)
        noff = pl.multiple_of(off + LANES, LANES)
        below = halves(nt(col_buf[lax.rem(b, 2), pl.ds(noff, LANES), :], xs[b]))
        b1 = b + 1
        block = sa[b1 // SPLITS, pl.ds(2 * lax.rem(b1, SPLITS), 2), :, :, pl.ds(noff, LANES)]
        done = (lo[0, pl.ds(noff, LANES), :], lo[1, pl.ds(noff, LANES), :])
        dg[...] = block.reshape(LANES, LANES) - nt_halves(done, done) - nt_halves(below, below)
        diag_inverse(block_of(dg[...]), store_inverse(b1))

    def own_rows(b):
        lanes = pl.ds(pl.multiple_of(b * LANES, LANES), LANES)
        found = nt_halves((po[0], po[1]), (lo[0, lanes, :], lo[1, lanes, :]))
        panel = nt(own_s[:, lanes] - found, xs[b])
        out_ref[:, lanes] = panel
        for i, half in enumerate(halves(panel)):
            po[i, :, lanes] = half

    second = range(SPLITS, 2 * SPLITS)
    agz_done(0)
    agz_done(1)
    agx_done(0)
    agz_done(2)
    agx_done(1)
    sib_done(0)
    col_buf[0] = sa[:, :, :, :, pl.ds(0, LANES)].reshape(n_cols, LANES)
    diag_inverse(block_of(col_buf[0, 0:LANES, :]), store_inverse(0))

    def before_0():
        @pl.when(at_y0)
        def _():
            for j in second:
                rsz_done(j)

        agz_done(3)
        agx_done(2)
        sib_done(1)

    def before_1():
        @pl.when(off_y0)
        def _():
            for j in second:
                agy_done(j)

        agx_done(3)
        sib_done(2)
        rs_hop(0)

    def before_2():
        for j in second:
            agz_done(j)
        sib_done(3)
        rs_hop(1)

    def before_3():
        for j in second:
            agx_done(j)
        sib_done(4)
        rs_hop(2)

    def before_4():
        sib_done(5)
        rs_hop(3)

    def before_5():
        sib_done(6)
        rs_hop(4)

    def step(b, carry):
        for k, fn in enumerate((before_0, before_1, before_2, before_3, before_4, before_5)):
            pl.when(b == k)(fn)
        next_diag(b)
        rest_of(b)
        return carry

    lax.fori_loop(0, 6, step, 0)
    sib_done(7)
    rs_hop(5)

    def own_schur(i):
        for q in range(PANELS * SPLITS):
            lanes = lanes_of(q)
            own_s[i * SHARE : (i + 1) * SHARE, lanes] = kern[i * SHARE : (i + 1) * SHARE, lanes] - t[q, mz, i, mx]

    pl.when(off_y0)(lambda: own_schur(0))
    for i in range(1, 4):
        own_schur(i)
    next_diag(6)
    rest_of(6)
    for b in range(8):
        own_rows(b)

    @pl.when(pos < NY - 1)
    def _():
        for c in range(CHUNKS):
            ring_chunk(c).wait_send()

    for c in range(CHUNKS):
        sib_chunk(c, core).wait_send()

    @pl.when(at_y0)
    def _():
        for k in range(1, NY):
            f_y(k).wait_send()

    for k in range(1, NZ):
        f_z(k, mz).wait_send()
    for k in range(1, NX):
        f_x(k, mx).wait_send()
    f_sib(core).wait_send()

    def drain_streams(rnd):
        for b in range(PANELS):
            for h in range(SPLITS):
                stream(b, h, rnd)[2]()

    pl.when(off_y0)(lambda: drain_streams(0))
    pl.when(at_y0)(lambda: drain_streams(1))
    for j in range(2 * SPLITS):
        @pl.when(at_y0)
        def _():
            for k in range(1, NX):
                rsx(j, k).wait_send()
            for k in range(1, NZ):
                rsz(j, k).wait_send()

            def sent():
                for k in range(1, NY):
                    agy(j, k).wait_send()

            gathers(j, sent)

        def sent_all():
            for k in range(1, NZ):
                agz(j, k, mz).wait_send()
            for k in range(1, NX):
                agx(j, k, mx).wait_send()
            for k in range(NX):
                ags(j, k, core).wait_send()

        gathers(j, sent_all)


def panels_of(lf, feats, wts):
    vmem = pl.BlockSpec(memory_space=pltpu.VMEM)
    anyspace = pl.BlockSpec(memory_space=pl.ANY)
    width = lf.shape[2] * lf.shape[3]
    fwidth = feats.shape[2]
    own, n = 4 * SHARE, PANELS * BLOCK
    dma = pltpu.SemaphoreType.DMA
    return pl.pallas_call(
        panels_kernel,
        out_shape=jax.ShapeDtypeStruct((own, n), F32),
        in_specs=[anyspace, vmem, vmem],
        out_specs=vmem,
        scratch_shapes=[
            pltpu.VMEM(lf.shape, BF16),
            pltpu.VMEM((SPLITS, 2 * CHUNK_ROWS, LANES), F32),
            pltpu.VMEM((4, BLOCK, width), BF16),
            pltpu.VMEM((PANELS, BLOCK, width), BF16),
            pltpu.VMEM((PANELS, NZ, NX, SHARE, fwidth), BF16),
            pltpu.VMEM((PANELS * SPLITS, NZ, 4, NX, SHARE, LANES), F32),
            pltpu.VMEM((own, n), F32),
            pltpu.VMEM((PANELS, 2, NZ - 1, 4, NX, SHARE, LANES), F32),
            pltpu.VMEM((PANELS, 2, NX - 1, NZ, 4, SHARE, LANES), F32),
            pltpu.VMEM((PANELS, 2, NX - 1, 4, SHARE, LANES), F32),
            pltpu.VMEM((PANELS, 2, NZ - 1, 4, SHARE, LANES), F32),
            pltpu.VMEM((PANELS * SPLITS, NX - 1, NZ, SHARE, LANES), F32),
            pltpu.VMEM((PANELS * SPLITS, NZ - 1, SHARE, LANES), F32),
            pltpu.VMEM((PANELS, NZ, NX, SHARE, n), F32),
            pltpu.VMEM((own, n), F32),
            pltpu.VMEM((2, n, n), BF16),
            pltpu.VMEM((n // LANES, LANES, LANES), F32),
            pltpu.VMEM((2, n, LANES), F32),
            pltpu.VMEM((LANES, LANES), F32),
            pltpu.VMEM((2, own, n), BF16),
            dma((2, CHUNKS)), dma((2, CHUNKS)),
            dma((14,)), dma((14,)),
            dma((PANELS * SPLITS, 10)), dma((PANELS * SPLITS, 10)),
            dma((PANELS * SPLITS, 27)), dma((PANELS * SPLITS, 27)),
            dma((4,)),
        ],
        compiler_params=pltpu.CompilerParams(
            collective_id=0, has_side_effects=True, vmem_limit_bytes=58 * 2**20
        ),
    )(lf, feats, wts)


def per_device(features, left_factor, ard_weights):
    lf = left_factor.reshape(4, BLOCK, 2, -1)
    feats = features.reshape(4, SHARE, -1)
    panels = panels_of(lf, feats, ard_weights.reshape(1, -1))
    return panels.reshape(4, 1, 1, SHARE, PANELS * BLOCK)


def solution(mesh):
    return jax.shard_map(
        per_device,
        mesh=mesh,
        in_specs=(P(None, "row", "col", None, None), P(None, "row", None, None, "col", None), P()),
        out_specs=P(None, "row", "col", None, None),
        check_vma=False,
    )
```

```python
import functools

import jax
import jax.numpy as jnp
from jax import lax
from jax.experimental import pallas as pl
from jax.experimental.pallas import tpu as pltpu
from jax.sharding import PartitionSpec as P

HIGHEST = lax.Precision.HIGHEST
MESH = pl.DeviceIdType.MESH
F32 = jnp.float32

NY, NX, NZ = 4, 4, 8
BLOCK = 512
PANELS = 2
SHARE = 16
LANES = 128
SPLITS = BLOCK // LANES
CHUNKS = 8
CHUNK_ROWS = BLOCK // CHUNKS
ROUNDS = ((0, 4), (1, 3))
HOPS = 6
BF16 = jnp.bfloat16


def nt(left, right, precision=HIGHEST):
    return lax.dot_general(
        left, right, (((1,), (1,)), ((), ())), precision=precision, preferred_element_type=F32
    )


def sub_row(tile, j):
    return jnp.broadcast_to(tile[j : j + 1, :], (8, LANES))


def lane_col(tile, j):
    return jnp.broadcast_to(tile[:, j : j + 1], (8, LANES))


def diag_inverse(load_tile, store_tile):
    rows = lax.broadcasted_iota(jnp.int32, (8, LANES), 0)
    lanes = lax.broadcasted_iota(jnp.int32, (8, LANES), 1)
    tiles = LANES // 8
    a = [load_tile(v) for v in range(tiles)]
    e = [jnp.where(lanes == rows + 8 * v, 1.0, 0.0).astype(F32) for v in range(tiles)]
    for g in range(tiles):
        c = [lane_col(a[g], 8 * g + j) for j in range(8)]
        ta, tb, tf = a[g], e[g], e[g]
        scale = jnp.zeros((8, LANES), F32)
        for j in range(8):
            pivot = sub_row(c[j], j)
            recip = 1.0 / pivot
            scale = jnp.where(rows == j, lax.rsqrt(pivot), scale)
            cj = c[j]
            both = jnp.where(rows == j, -1.0, cj)
            below = jnp.where(rows > j, cj, 0.0)

            def step(tile):
                return jnp.where(rows == j, 0.0, tile) - (both * sub_row(tile, j)) * recip

            for k in range(j + 1, 8):
                c[k] = step(c[k])
            if g < tiles - 1:
                ta, tb = step(ta), step(tb)
            tf = tf - (below * sub_row(tf, j)) * recip
        store_tile(g, tf * scale)
        if g < tiles - 1:
            wa = [sub_row(ta, j) for j in range(8)]
            wb = [sub_row(tb, j) for j in range(8)]
            for v in range(g + 1, tiles):
                m = [lane_col(a[v], 8 * g + j) for j in range(8)]

                def less(tile, w):
                    p = [m[j] * w[j] for j in range(8)]
                    return tile - (((p[0] + p[1]) + (p[2] + p[3])) + ((p[4] + p[5]) + (p[6] + p[7])))

                a[v] = less(a[v], wa)
                e[v] = less(e[v], wb)


def halves(value):
    high = value.astype(BF16)
    return high, (value - high.astype(F32)).astype(BF16)


def nt_halves(left, right):
    return nt(left[0], right[0], None) + (nt(left[0], right[1], None) + nt(left[1], right[0], None))


def ring_add(m, k, n):
    return lax.rem(m + (k + n), n)


def panels_kernel(
    lf_in, feats, wts, out_ref,
    raw, rt, lf, pan, fp, t, kern, bz1, bx1, bx2, bz2, rx, rz, sa, own_s,
    lo, xs, col_buf, dg, dacc, po,
    pan_s, pan_r, ft_s, ft_r, rs_s, rs_r, dg_s, dg_r, loc,
):
    row, col = lax.axis_index("row"), lax.axis_index("col")
    y, core = row // 2, lax.rem(row, 2)
    mz, mx = col // NX, lax.rem(col, NX)
    at_y0 = y == 0
    off_y0 = jnp.logical_not(at_y0)
    n_cols = PANELS * BLOCK

    def dev(dy=0, dx=0, dz=0, other=False):
        yy, xx, zz = ring_add(y, dy, NY), ring_add(mx, dx, NX), ring_add(mz, dz, NZ)
        cc = 1 - core if other else core
        return (yy * 2 + cc, zz * NX + xx)

    yp, ym = dev(dy=1), dev(dy=-1)
    zp, zm = dev(dz=1), dev(dz=-1)
    xp, xm = dev(dx=1), dev(dx=-1)
    sib = dev(other=True)

    def rcopy(src, dst, ssem, rsem, target):
        return pltpu.make_async_remote_copy(
            src_ref=src, dst_ref=dst, send_sem=ssem, recv_sem=rsem,
            device_id=target, device_id_type=MESH,
        )

    raw_copies = [pltpu.make_async_copy(lf_in.at[i], raw.at[i], loc.at[i]) for i in range(4)]
    for copy in raw_copies:
        copy.start()
    barrier = pltpu.get_barrier_semaphore()
    peers = [dev(dz=k) for k in range(1, NZ)] + [dev(dx=k) for k in range(1, NX)]
    peers += [dev(dy=k) for k in range(1, NY)] + [sib]
    for target in peers:
        pl.semaphore_signal(barrier, inc=1, device_id=target, device_id_type=MESH)

    def relayout(i, c, stores):
        rows = pl.ds(c * CHUNK_ROWS, CHUNK_ROWS)
        value = raw[i, rows].astype(F32).reshape(2 * CHUNK_ROWS, BLOCK)
        for lane in range(SPLITS):
            rt[lane] = value[:, lane * LANES : (lane + 1) * LANES]
        for j in range(2):
            for lane in range(SPLITS):
                part = rt[lane, pl.ds(j, CHUNK_ROWS, stride=2), :].astype(BF16)
                lanes = pl.ds(j * BLOCK + lane * LANES, LANES)
                for store in stores:
                    store(rows, lanes, part)

    def to_lf(i):
        def store(rows, lanes, part):
            lf[i, rows, lanes] = part

        return store

    def to_pan(rows, lanes, part):
        pan[core, rows, lanes] = part

    def relayout_blocks(first):
        def go(k, carry):
            i, c = first + k // CHUNKS, lax.rem(k, CHUNKS)
            relayout(i, c, [to_lf(i)])
            return carry

        lax.fori_loop(0, (4 - first) * CHUNKS, go, 0)

    pos = jnp.where(core == 0, y, ring_add(0, NY - y, NY))
    onward = (jnp.where(core == 0, yp[0], ym[0]), col)

    def pan_ref(b, c):
        return pan.at[b, pl.ds(c * CHUNK_ROWS, CHUNK_ROWS)]

    def ring_chunk(c):
        return rcopy(pan_ref(core, c), pan_ref(core, c), pan_s.at[0, c], pan_r.at[0, c], onward)

    def sib_chunk(c, b):
        return rcopy(pan_ref(b, c), pan_ref(b, c), pan_s.at[1, c], pan_r.at[1, c], sib)

    def f_slab():
        return fp.at[core, mz, mx]

    def f_y(k):
        return rcopy(f_slab(), f_slab(), ft_s.at[k - 1], ft_r.at[0], dev(dy=k))

    def f_z(k, z):
        ref = fp.at[core, z, mx]
        return rcopy(ref, ref, ft_s.at[2 + k], ft_r.at[2 + k], dev(dz=k))

    def f_x(k, x):
        ref = fp.at[core, :, x]
        return rcopy(ref, ref, ft_s.at[9 + k], ft_r.at[9 + k], dev(dx=k))

    def f_sib(b):
        return rcopy(fp.at[b], fp.at[b], ft_s.at[13], ft_r.at[13], sib)

    def f_z_start():
        for k in range(1, NZ):
            f_z(k, mz).start()

    def f_x_start():
        for k in range(1, NZ):
            f_z(k, ring_add(mz, -k, NZ)).wait_recv()
        for k in range(1, NX):
            f_x(k, mx).start()

    def f_sib_start():
        for k in range(1, NX):
            f_x(k, ring_add(mx, -k, NX)).wait_recv()
        f_sib(core).start()

    def stream(b, h, rnd):
        i0, ni = ROUNDS[rnd]
        isl = pl.ds(i0, ni)
        q = b * SPLITS + h
        w = h // 2
        z_first = h % 2 == 0
        sign = 1 if w == 0 else -1

        def part(axis, k):
            if z_first:
                return t.at[q, k, isl] if axis == "z" else t.at[q, mz, isl, k]
            return t.at[q, :, isl, k] if axis == "x" else t.at[q, k, isl, mx]

        def slot(axis, s):
            if z_first:
                return bz1.at[b, w, s, isl] if axis == "z" else bx2.at[b, w, s, isl]
            return bx1.at[b, w, s, :, isl] if axis == "x" else bz2.at[b, w, s, isl]

        order = ("z", "x") if z_first else ("x", "z")
        size = {
            "z": (NZ, mz) + ((zp, zm) if sign > 0 else (zm, zp)),
            "x": (NX, mx) + ((xp, xm) if sign > 0 else (xm, xp)),
        }
        base = {order[0]: 0, order[1]: size[order[0]][0] - 1}

        def copy(axis, src, s, target):
            i = base[axis] + s
            return rcopy(src, slot(axis, s), rs_s.at[q, i], rs_r.at[q, i], target)

        def begin(axis):
            n, m, plus, minus = size[axis]
            hp, hm = n // 2, n // 2 - 1
            copy(axis, part(axis, ring_add(m, sign * hp, n)), 0, plus).start()
            copy(axis, part(axis, ring_add(m, -sign * hm, n)), hp, minus).start()

        def hop(axis, s):
            n, m, plus, minus = size[axis]
            hp, hm = n // 2, n // 2 - 1
            here = slot(axis, s)
            copy(axis, here, s, plus).wait_recv()
            if s < hp - 1:
                here[...] = here[...] + part(axis, ring_add(m, sign * (hp - 1 - s), n))[...]
                copy(axis, here, s + 1, plus).start()
            if s < hm:
                there = slot(axis, hp + s)
                copy(axis, there, hp + s, minus).wait_recv()
                if s < hm - 1:
                    there[...] = there[...] + part(axis, ring_add(m, sign * (s + 1 - hm), n))[...]
                    copy(axis, there, hp + s + 1, minus).start()
            if s == hp - 1:
                mine = part(axis, m)
                mine[...] = mine[...] + (here[...] + slot(axis, hp + hm - 1)[...])
                if axis == order[0]:
                    begin(order[1])

        def macro(g):
            first = size[order[0]][0] // 2
            if g < first:
                hop(order[0], g)
            else:
                hop(order[1], g - first)

        def drain():
            for axis in order:
                n, m, plus, minus = size[axis]
                for s in range(n - 1):
                    copy(axis, slot(axis, s), s, plus).wait_send()

        return (lambda: begin(order[0])), macro, drain

    def rs_hop(g, kind):
        def go(rnd):
            for b in (core, 1 - core):
                for h in range(kind, SPLITS, 2):
                    stream(b, h, rnd)[1](g)

        pl.when(off_y0)(lambda: go(0))
        pl.when(at_y0)(lambda: go(1))

    def product(b, pair, i):
        rows = nt(lf[i], pan[b, pair * 2 * LANES : (pair + 1) * 2 * LANES, :], None)
        for u in range(2):
            q = b * SPLITS + pair * 2 + u
            t[q, :, i] = rows[:, u * LANES : (u + 1) * LANES].reshape(NZ, NX, SHARE, LANES)

    def lanes_of(j):
        return pl.ds(j * LANES, LANES)

    def dcopy(src, dst, j, i, target):
        return rcopy(src, dst, dg_s.at[j, i], dg_r.at[j, i], target)

    def rsx(j, k):
        return dcopy(t.at[j, :, 0, ring_add(mx, k, NX)], rx.at[j, k - 1], j, k - 1, dev(dx=k))

    def rsz(j, k):
        return dcopy(t.at[j, ring_add(mz, k, NZ), 0, mx], rz.at[j, k - 1], j, 2 + k, dev(dz=k))

    def agy(j, k):
        ref = sa.at[core, mz, mx, :, lanes_of(j)]
        return rcopy(ref, ref, dg_s.at[j, 9 + k], dg_r.at[j, 10], dev(dy=k))

    def agz(j, k, z):
        ref = sa.at[core, z, mx, :, lanes_of(j)]
        return dcopy(ref, ref, j, 12 + k, dev(dz=k))

    def agx(j, k, x):
        ref = sa.at[core, :, x, :, lanes_of(j)]
        return dcopy(ref, ref, j, 19 + k, dev(dx=k))

    def ags(j, k, b):
        ref = sa.at[b, :, ring_add(mx, -k, NX), :, lanes_of(j)]
        return dcopy(ref, ref, j, 23 + k, sib)

    def gathers(j, fn):
        if j < SPLITS:
            fn()
        else:
            pl.when(core == 1)(fn)

    def rsx_start(j):
        for k in range(1, NX):
            rsx(j, k).start()

    def rsx_done(j):
        for k in range(1, NX):
            rsx(j, k).wait_recv()
        total = t[j, :, 0, mx] + rx[j, 0]
        t[j, :, 0, mx] = total + (rx[j, 1] + rx[j, 2])
        for k in range(1, NZ):
            rsz(j, k).start()

    def rsz_done(j):
        for k in range(1, NZ):
            rsz(j, k).wait_recv()
        total = t[j, mz, 0, mx] + rz[j, 0]
        for k in range(1, NZ - 1, 2):
            total = total + (rz[j, k] + rz[j, k + 1])
        lanes = lanes_of(j)
        schur = kern[0:SHARE, lanes] - total
        own_s[0:SHARE, lanes] = schur

        def send():
            sa[core, mz, mx, :, lanes] = schur
            for k in range(1, NY):
                agy(j, k).start()
            for k in range(1, NZ):
                agz(j, k, mz).start()

        gathers(j, send)

    def agy_done(j):
        def go():
            agy(j, 1).wait_recv()
            for k in range(1, NZ):
                agz(j, k, mz).start()

        gathers(j, go)

    def agz_done(j):
        def go():
            for k in range(1, NZ):
                agz(j, k, ring_add(mz, -k, NZ)).wait_recv()
            for k in range(1, NX):
                agx(j, k, mx).start()
            ags(j, 0, core).start()

        gathers(j, go)

    def agx_done(j):
        def go():
            for k in range(1, NX):
                agx(j, k, ring_add(mx, -k, NX)).wait_recv()
                ags(j, k, core).start()

        gathers(j, go)

    def sib_done(j):
        def go():
            for k in range(NX):
                ags(j, k, 1 - core).wait_recv()

        if j < SPLITS:
            go()
        else:
            pl.when(core == 0)(go)

    def own_kernel():
        weights = wts[...]
        own_feat = feats[...].reshape(4 * SHARE, -1).astype(F32) * weights
        own_norm = jnp.sum(own_feat * own_feat, axis=1, keepdims=True)
        ids = lax.broadcasted_iota(jnp.int32, (4 * SHARE, BLOCK), 0)
        row_ids = ((ids // SHARE) * 8 + row) * BLOCK + col * SHARE + lax.rem(ids, SHARE)
        for b in range(PANELS):
            feat = fp[b].reshape(BLOCK, -1).astype(F32) * weights
            norm = nt(jnp.ones((8, feat.shape[1]), F32), feat * feat)[0:1, :]
            dist = own_norm + norm - 2.0 * nt(own_feat, feat)
            cols = lax.broadcasted_iota(jnp.int32, (4 * SHARE, BLOCK), 1) + b * BLOCK
            jitter = jnp.where(row_ids == cols, 0.01, 0.0).astype(F32)
            kern[:, b * BLOCK : (b + 1) * BLOCK] = jnp.exp(-0.5 * dist) + jitter

    @pl.when(at_y0)
    def _():
        fp[core, mz, mx] = feats[0]

    raw_copies[0].wait()
    pl.semaphore_wait(barrier, len(peers))

    @pl.when(at_y0)
    def _():
        for k in range(1, NY):
            f_y(k).start()
        f_z_start()
        for c in range(CHUNKS):
            relayout(0, c, [to_lf(0), to_pan])
            sib_chunk(c, core).start()
            ring_chunk(c).start()

    lo[...] = jnp.zeros(lo.shape, BF16)
    po[...] = jnp.zeros(po.shape, BF16)
    xs[7] = jnp.zeros((LANES, LANES), F32)
    dacc[...] = jnp.zeros((LANES, LANES), F32)
    col_buf[1] = jnp.zeros((n_cols, LANES), F32)
    sa[0, :, :, :, pl.ds(BLOCK, BLOCK)] = jnp.zeros((NZ, NX, SHARE, BLOCK), F32)
    for copy in raw_copies[1:]:
        copy.wait()

    def begin(b, hs, rnd):
        for h in hs:
            stream(b, h, rnd)[0]()

    @pl.when(at_y0)
    def _():
        for pair in range(2):
            for c in range(4 * pair, 4 * pair + 4):
                sib_chunk(c, 1 - core).wait_recv()
            product(0, pair, 0)
            rsx_start(2 * pair)
            rsx_start(2 * pair + 1)
        relayout_blocks(1)

        def rest(b):
            def go(i, carry):
                product(b, 0, i)
                product(b, 1, i)
                return carry

            lax.fori_loop(1, 4, go, 0)

        rest(0)
        begin(0, (0, 2), 1)
        f_x_start()
        product(1, 0, 0)
        product(1, 1, 0)
        for j in range(SPLITS):
            rsx_done(j)
        for j in range(SPLITS, 2 * SPLITS):
            rsx_start(j)
        rest(1)
        begin(1, (0, 2), 1)
        f_sib_start()
        f_sib(1 - core).wait_recv()
        own_kernel()
        for j in range(SPLITS):
            rsz_done(j)
        begin(0, (1, 3), 1)
        begin(1, (1, 3), 1)

    @pl.when(off_y0)
    def _():
        relayout_blocks(0)
        f_y(1).wait_recv()
        f_z_start()

        def whole(b, pair):
            def go(i, carry):
                product(b, pair, i)
                return carry

            lax.fori_loop(0, 4, go, 0)
            begin(b, (2 * pair, 2 * pair + 1), 0)

        for c in range(CHUNKS):
            ring_chunk(c).wait_recv()

            @pl.when(pos < NY - 1)
            def _():
                ring_chunk(c).start()

            sib_chunk(c, core).start()
            if c == 3:
                whole(core, 0)
                f_x_start()
        whole(core, 1)
        f_sib_start()
        for pair in range(2):
            for c in range(4 * pair, 4 * pair + 4):
                sib_chunk(c, 1 - core).wait_recv()
            whole(1 - core, pair)
        f_sib(1 - core).wait_recv()
        own_kernel()
        for j in range(SPLITS):
            agy_done(j)

    def store_inverse(b):
        def store(g, tile):
            xs[b, 8 * g : 8 * g + 8, :] = tile

        return store

    def block_of(value):
        return lambda v: value[8 * v : 8 * v + 8, :]

    def step(b):
        prev, after = lax.rem(b + 7, 8), lax.rem(b + 1, 8)
        here = pl.ds(pl.multiple_of(b * LANES, LANES), LANES)
        back = pl.ds(pl.multiple_of(prev * LANES, LANES), LANES)
        ahead = pl.ds(pl.multiple_of(after * LANES, LANES), LANES)
        last = col_buf.at[lax.rem(b + 1, 2)]
        corner = halves(nt(last[here, :], xs[prev]))
        block = sa[b // SPLITS, pl.ds(2 * lax.rem(b, SPLITS), 2), :, :, here]
        dg[...] = block.reshape(LANES, LANES) - dacc[...] - nt_halves(corner, corner)
        diag_inverse(block_of(dg[...]), store_inverse(b))
        for i, half in enumerate(halves(nt(last[...], xs[prev]))):
            lo[i, :, back] = half
        update = nt_halves((lo[0], lo[1]), (lo[0, here, :], lo[1, here, :]))
        col_buf[lax.rem(b, 2)] = sa[:, :, :, :, here].reshape(n_cols, LANES) - update
        below = (lo[0, ahead, :], lo[1, ahead, :])
        dacc[...] = nt_halves(below, below)

    def own_rows(b):
        lanes = pl.ds(pl.multiple_of(b * LANES, LANES), LANES)
        found = nt_halves((po[0], po[1]), (lo[0, lanes, :], lo[1, lanes, :]))
        panel = nt(own_s[:, lanes] - found, xs[b])
        out_ref[:, lanes] = panel
        for i, half in enumerate(halves(panel)):
            po[i, :, lanes] = half

    second = range(SPLITS, 2 * SPLITS)
    rs_hop(0, 0)
    agz_done(0)
    agz_done(1)
    agx_done(0)
    agz_done(2)
    agx_done(1)
    sib_done(0)

    def before_0():
        @pl.when(at_y0)
        def _():
            for j in second:
                rsx_done(j)

        rs_hop(1, 0)

    def before_1():
        agz_done(3)
        agx_done(2)
        sib_done(1)

        @pl.when(at_y0)
        def _():
            for j in second:
                rsz_done(j)

        rs_hop(0, 1)

    def before_2():
        agx_done(3)
        sib_done(2)

        @pl.when(off_y0)
        def _():
            for j in second:
                agy_done(j)

        rs_hop(2, 0)

    def before_3():
        sib_done(3)
        for j in second:
            agz_done(j)
        rs_hop(1, 1)

    def before_4():
        for j in second:
            agx_done(j)
        sib_done(4)
        rs_hop(3, 0)
        rs_hop(2, 1)

    def before_5():
        sib_done(5)
        rs_hop(4, 0)
        rs_hop(3, 1)

    def before_6():
        sib_done(6)
        rs_hop(5, 0)
        rs_hop(4, 1)

    def round_of(b, carry):
        before = (before_0, before_1, before_2, before_3, before_4, before_5, before_6)
        for k, fn in enumerate(before):
            pl.when(b == k)(fn)
        step(b)
        return carry

    lax.fori_loop(0, 7, round_of, 0)
    sib_done(7)
    rs_hop(5, 1)

    def own_schur(i):
        for q in range(PANELS * SPLITS):
            lanes = lanes_of(q)
            own_s[i * SHARE : (i + 1) * SHARE, lanes] = kern[i * SHARE : (i + 1) * SHARE, lanes] - t[q, mz, i, mx]

    pl.when(off_y0)(lambda: own_schur(0))
    for i in range(1, 4):
        own_schur(i)
    step(7)
    for b in range(8):
        own_rows(b)

    @pl.when(pos < NY - 1)
    def _():
        for c in range(CHUNKS):
            ring_chunk(c).wait_send()

    for c in range(CHUNKS):
        sib_chunk(c, core).wait_send()

    @pl.when(at_y0)
    def _():
        for k in range(1, NY):
            f_y(k).wait_send()

    for k in range(1, NZ):
        f_z(k, mz).wait_send()
    for k in range(1, NX):
        f_x(k, mx).wait_send()
    f_sib(core).wait_send()

    def drain_streams(rnd):
        for b in range(PANELS):
            for h in range(SPLITS):
                stream(b, h, rnd)[2]()

    pl.when(off_y0)(lambda: drain_streams(0))
    pl.when(at_y0)(lambda: drain_streams(1))
    for j in range(2 * SPLITS):
        @pl.when(at_y0)
        def _():
            for k in range(1, NX):
                rsx(j, k).wait_send()
            for k in range(1, NZ):
                rsz(j, k).wait_send()

            def sent():
                for k in range(1, NY):
                    agy(j, k).wait_send()

            gathers(j, sent)

        def sent_all():
            for k in range(1, NZ):
                agz(j, k, mz).wait_send()
            for k in range(1, NX):
                agx(j, k, mx).wait_send()
            for k in range(NX):
                ags(j, k, core).wait_send()

        gathers(j, sent_all)


def panels_of(lf, feats, wts):
    vmem = pl.BlockSpec(memory_space=pltpu.VMEM)
    anyspace = pl.BlockSpec(memory_space=pl.ANY)
    width = lf.shape[2] * lf.shape[3]
    fwidth = feats.shape[2]
    own, n = 4 * SHARE, PANELS * BLOCK
    dma = pltpu.SemaphoreType.DMA
    return pl.pallas_call(
        panels_kernel,
        out_shape=jax.ShapeDtypeStruct((own, n), F32),
        in_specs=[anyspace, vmem, vmem],
        out_specs=vmem,
        scratch_shapes=[
            pltpu.VMEM(lf.shape, BF16),
            pltpu.VMEM((SPLITS, 2 * CHUNK_ROWS, LANES), F32),
            pltpu.VMEM((4, BLOCK, width), BF16),
            pltpu.VMEM((PANELS, BLOCK, width), BF16),
            pltpu.VMEM((PANELS, NZ, NX, SHARE, fwidth), BF16),
            pltpu.VMEM((PANELS * SPLITS, NZ, 4, NX, SHARE, LANES), F32),
            pltpu.VMEM((own, n), F32),
            pltpu.VMEM((PANELS, 2, NZ - 1, 4, NX, SHARE, LANES), F32),
            pltpu.VMEM((PANELS, 2, NX - 1, NZ, 4, SHARE, LANES), F32),
            pltpu.VMEM((PANELS, 2, NX - 1, 4, SHARE, LANES), F32),
            pltpu.VMEM((PANELS, 2, NZ - 1, 4, SHARE, LANES), F32),
            pltpu.VMEM((PANELS * SPLITS, NX - 1, NZ, SHARE, LANES), F32),
            pltpu.VMEM((PANELS * SPLITS, NZ - 1, SHARE, LANES), F32),
            pltpu.VMEM((PANELS, NZ, NX, SHARE, n), F32),
            pltpu.VMEM((own, n), F32),
            pltpu.VMEM((2, n, n), BF16),
            pltpu.VMEM((n // LANES, LANES, LANES), F32),
            pltpu.VMEM((2, n, LANES), F32),
            pltpu.VMEM((LANES, LANES), F32),
            pltpu.VMEM((LANES, LANES), F32),
            pltpu.VMEM((2, own, n), BF16),
            dma((2, CHUNKS)), dma((2, CHUNKS)),
            dma((14,)), dma((14,)),
            dma((PANELS * SPLITS, 10)), dma((PANELS * SPLITS, 10)),
            dma((PANELS * SPLITS, 27)), dma((PANELS * SPLITS, 27)),
            dma((4,)),
        ],
        compiler_params=pltpu.CompilerParams(
            collective_id=0, has_side_effects=True, vmem_limit_bytes=58 * 2**20
        ),
    )(lf, feats, wts)


def per_device(features, left_factor, ard_weights):
    lf = left_factor.reshape(4, BLOCK, 2, -1)
    feats = features.reshape(4, SHARE, -1)
    panels = panels_of(lf, feats, ard_weights.reshape(1, -1))
    return panels.reshape(4, 1, 1, SHARE, PANELS * BLOCK)


def solution(mesh):
    return jax.shard_map(
        per_device,
        mesh=mesh,
        in_specs=(P(None, "row", "col", None, None), P(None, "row", None, None, "col", None), P()),
        out_specs=P(None, "row", "col", None, None),
        check_vma=False,
    )
```

```python
import functools

import jax
import jax.numpy as jnp
from jax import lax
from jax.experimental import pallas as pl
from jax.experimental.pallas import tpu as pltpu
from jax.sharding import PartitionSpec as P

HIGHEST = lax.Precision.HIGHEST
MESH = pl.DeviceIdType.MESH
F32 = jnp.float32

NY, NX, NZ = 4, 4, 8
BLOCK = 512
PANELS = 2
SHARE = 16
LANES = 128
SPLITS = BLOCK // LANES
CHUNKS = 8
CHUNK_ROWS = BLOCK // CHUNKS
ROUNDS = ((0, 4), (1, 3))
HOPS = 6
BF16 = jnp.bfloat16


def nt(left, right, precision=HIGHEST):
    return lax.dot_general(
        left, right, (((1,), (1,)), ((), ())), precision=precision, preferred_element_type=F32
    )


def sub_row(tile, j):
    return jnp.broadcast_to(tile[j : j + 1, :], (8, LANES))


def lane_col(tile, j):
    return jnp.broadcast_to(tile[:, j : j + 1], (8, LANES))


def diag_inverse(load_tile, store_tile):
    rows = lax.broadcasted_iota(jnp.int32, (8, LANES), 0)
    lanes = lax.broadcasted_iota(jnp.int32, (8, LANES), 1)
    tiles = LANES // 8
    a = [load_tile(v) for v in range(tiles)]
    e = [jnp.where(lanes == rows + 8 * v, 1.0, 0.0).astype(F32) for v in range(tiles)]
    for g in range(tiles):
        c = [lane_col(a[g], 8 * g + j) for j in range(8)]
        pivots = [sub_row(c[k], k) for k in range(8)]
        ta, tb, tf = a[g], e[g], e[g]
        scale = jnp.zeros((8, LANES), F32)
        for j in range(8):
            pivot = pivots[j]
            recip = 1.0 / pivot
            scale = jnp.where(rows == j, lax.rsqrt(pivot), scale)
            cj = c[j]
            both = jnp.where(rows == j, -1.0, cj)
            below = jnp.where(rows > j, cj, 0.0)

            def step(tile):
                return jnp.where(rows == j, 0.0, tile) - (both * sub_row(tile, j)) * recip

            for k in range(j + 1, 8):
                unit = sub_row(c[k], j)
                pivots[k] = pivots[k] - (unit * unit) * recip
                c[k] = jnp.where(rows == j, 0.0, c[k]) - (both * unit) * recip
            if g < tiles - 1:
                ta, tb = step(ta), step(tb)
            tf = tf - (below * sub_row(tf, j)) * recip
        store_tile(g, tf * scale)
        if g < tiles - 1:
            wa = [sub_row(ta, j) for j in range(8)]
            wb = [sub_row(tb, j) for j in range(8)]
            for v in range(g + 1, tiles):
                m = [lane_col(a[v], 8 * g + j) for j in range(8)]

                def less(tile, w):
                    p = [m[j] * w[j] for j in range(8)]
                    return tile - (((p[0] + p[1]) + (p[2] + p[3])) + ((p[4] + p[5]) + (p[6] + p[7])))

                a[v] = less(a[v], wa)
                e[v] = less(e[v], wb)


def halves(value):
    high = value.astype(BF16)
    return high, (value - high.astype(F32)).astype(BF16)


def nt_halves(left, right):
    return nt(left[0], right[0], None) + (nt(left[0], right[1], None) + nt(left[1], right[0], None))


def ring_add(m, k, n):
    return lax.rem(m + (k + n), n)


def panels_kernel(
    lf_in, feats, wts, out_ref,
    raw, rt, lf, pan, fp, t, kern, bz1, bx1, bx2, bz2, rx, rz, sa, own_s,
    lo, xs, col_buf, dg, dacc, po,
    pan_s, pan_r, ft_s, ft_r, rs_s, rs_r, dg_s, dg_r, loc,
):
    row, col = lax.axis_index("row"), lax.axis_index("col")
    y, core = row // 2, lax.rem(row, 2)
    mz, mx = col // NX, lax.rem(col, NX)
    at_y0 = y == 0
    off_y0 = jnp.logical_not(at_y0)
    n_cols = PANELS * BLOCK

    def dev(dy=0, dx=0, dz=0, other=False):
        yy, xx, zz = ring_add(y, dy, NY), ring_add(mx, dx, NX), ring_add(mz, dz, NZ)
        cc = 1 - core if other else core
        return (yy * 2 + cc, zz * NX + xx)

    yp, ym = dev(dy=1), dev(dy=-1)
    zp, zm = dev(dz=1), dev(dz=-1)
    xp, xm = dev(dx=1), dev(dx=-1)
    sib = dev(other=True)

    def rcopy(src, dst, ssem, rsem, target):
        return pltpu.make_async_remote_copy(
            src_ref=src, dst_ref=dst, send_sem=ssem, recv_sem=rsem,
            device_id=target, device_id_type=MESH,
        )

    raw_copies = [pltpu.make_async_copy(lf_in.at[i], raw.at[i], loc.at[i]) for i in range(4)]
    for copy in raw_copies:
        copy.start()
    barrier = pltpu.get_barrier_semaphore()
    peers = [dev(dz=k) for k in range(1, NZ)] + [dev(dx=k) for k in range(1, NX)]
    peers += [dev(dy=k) for k in range(1, NY)] + [sib]
    for target in peers:
        pl.semaphore_signal(barrier, inc=1, device_id=target, device_id_type=MESH)

    def relayout(i, c, stores):
        rows = pl.ds(c * CHUNK_ROWS, CHUNK_ROWS)
        value = raw[i, rows].astype(F32).reshape(2 * CHUNK_ROWS, BLOCK)
        for lane in range(SPLITS):
            rt[lane] = value[:, lane * LANES : (lane + 1) * LANES]
        for j in range(2):
            for lane in range(SPLITS):
                part = rt[lane, pl.ds(j, CHUNK_ROWS, stride=2), :].astype(BF16)
                lanes = pl.ds(j * BLOCK + lane * LANES, LANES)
                for store in stores:
                    store(rows, lanes, part)

    def to_lf(i):
        def store(rows, lanes, part):
            lf[i, rows, lanes] = part

        return store

    def to_pan(rows, lanes, part):
        pan[core, rows, lanes] = part

    def relayout_blocks(first):
        def go(k, carry):
            i, c = first + k // CHUNKS, lax.rem(k, CHUNKS)
            relayout(i, c, [to_lf(i)])
            return carry

        lax.fori_loop(0, (4 - first) * CHUNKS, go, 0)

    pos = jnp.where(core == 0, y, ring_add(0, NY - y, NY))
    onward = (jnp.where(core == 0, yp[0], ym[0]), col)

    def pan_ref(b, c):
        return pan.at[b, pl.ds(c * CHUNK_ROWS, CHUNK_ROWS)]

    def ring_chunk(c):
        return rcopy(pan_ref(core, c), pan_ref(core, c), pan_s.at[0, c], pan_r.at[0, c], onward)

    def sib_chunk(c, b):
        return rcopy(pan_ref(b, c), pan_ref(b, c), pan_s.at[1, c], pan_r.at[1, c], sib)

    def f_slab():
        return fp.at[core, mz, mx]

    def f_y(k):
        return rcopy(f_slab(), f_slab(), ft_s.at[k - 1], ft_r.at[0], dev(dy=k))

    def f_z(k, z):
        ref = fp.at[core, z, mx]
        return rcopy(ref, ref, ft_s.at[2 + k], ft_r.at[2 + k], dev(dz=k))

    def f_x(k, x):
        ref = fp.at[core, :, x]
        return rcopy(ref, ref, ft_s.at[9 + k], ft_r.at[9 + k], dev(dx=k))

    def f_sib(b):
        return rcopy(fp.at[b], fp.at[b], ft_s.at[13], ft_r.at[13], sib)

    def f_z_start():
        for k in range(1, NZ):
            f_z(k, mz).start()

    def f_x_start():
        for k in range(1, NZ):
            f_z(k, ring_add(mz, -k, NZ)).wait_recv()
        for k in range(1, NX):
            f_x(k, mx).start()

    def f_sib_start():
        for k in range(1, NX):
            f_x(k, ring_add(mx, -k, NX)).wait_recv()
        f_sib(core).start()

    def stream(b, h, rnd):
        i0, ni = ROUNDS[rnd]
        isl = pl.ds(i0, ni)
        q = b * SPLITS + h
        w = h // 2
        z_first = h % 2 == 0
        sign = 1 if w == 0 else -1

        def part(axis, k):
            if z_first:
                return t.at[q, k, isl] if axis == "z" else t.at[q, mz, isl, k]
            return t.at[q, :, isl, k] if axis == "x" else t.at[q, k, isl, mx]

        def slot(axis, s):
            if z_first:
                return bz1.at[b, w, s, isl] if axis == "z" else bx2.at[b, w, s, isl]
            return bx1.at[b, w, s, :, isl] if axis == "x" else bz2.at[b, w, s, isl]

        order = ("z", "x") if z_first else ("x", "z")
        size = {
            "z": (NZ, mz) + ((zp, zm) if sign > 0 else (zm, zp)),
            "x": (NX, mx) + ((xp, xm) if sign > 0 else (xm, xp)),
        }
        base = {order[0]: 0, order[1]: size[order[0]][0] - 1}

        def copy(axis, src, s, target):
            i = base[axis] + s
            return rcopy(src, slot(axis, s), rs_s.at[q, i], rs_r.at[q, i], target)

        def begin(axis):
            n, m, plus, minus = size[axis]
            hp, hm = n // 2, n // 2 - 1
            copy(axis, part(axis, ring_add(m, sign * hp, n)), 0, plus).start()
            copy(axis, part(axis, ring_add(m, -sign * hm, n)), hp, minus).start()

        def hop(axis, s):
            n, m, plus, minus = size[axis]
            hp, hm = n // 2, n // 2 - 1
            here = slot(axis, s)
            copy(axis, here, s, plus).wait_recv()
            if s < hp - 1:
                here[...] = here[...] + part(axis, ring_add(m, sign * (hp - 1 - s), n))[...]
                copy(axis, here, s + 1, plus).start()
            if s < hm:
                there = slot(axis, hp + s)
                copy(axis, there, hp + s, minus).wait_recv()
                if s < hm - 1:
                    there[...] = there[...] + part(axis, ring_add(m, sign * (s + 1 - hm), n))[...]
                    copy(axis, there, hp + s + 1, minus).start()
            if s == hp - 1:
                mine = part(axis, m)
                mine[...] = mine[...] + (here[...] + slot(axis, hp + hm - 1)[...])
                if axis == order[0]:
                    begin(order[1])

        def macro(g):
            first = size[order[0]][0] // 2
            if g < first:
                hop(order[0], g)
            else:
                hop(order[1], g - first)

        def drain():
            for axis in order:
                n, m, plus, minus = size[axis]
                for s in range(n - 1):
                    copy(axis, slot(axis, s), s, plus).wait_send()

        return (lambda: begin(order[0])), macro, drain

    def rs_hop(g, kind):
        def go(rnd):
            for b in (core, 1 - core):
                for h in range(kind, SPLITS, 2):
                    stream(b, h, rnd)[1](g)

        pl.when(off_y0)(lambda: go(0))
        pl.when(at_y0)(lambda: go(1))

    def product(b, pair, i):
        rows = nt(lf[i], pan[b, pair * 2 * LANES : (pair + 1) * 2 * LANES, :], None)
        for u in range(2):
            q = b * SPLITS + pair * 2 + u
            t[q, :, i] = rows[:, u * LANES : (u + 1) * LANES].reshape(NZ, NX, SHARE, LANES)

    def lanes_of(j):
        return pl.ds(j * LANES, LANES)

    def dcopy(src, dst, j, i, target):
        return rcopy(src, dst, dg_s.at[j, i], dg_r.at[j, i], target)

    def rsx(j, k):
        return dcopy(t.at[j, :, 0, ring_add(mx, k, NX)], rx.at[j, k - 1], j, k - 1, dev(dx=k))

    def rsz(j, k):
        return dcopy(t.at[j, ring_add(mz, k, NZ), 0, mx], rz.at[j, k - 1], j, 2 + k, dev(dz=k))

    def agy(j, k):
        ref = sa.at[core, mz, mx, :, lanes_of(j)]
        return rcopy(ref, ref, dg_s.at[j, 9 + k], dg_r.at[j, 10], dev(dy=k))

    def agz(j, k, z):
        ref = sa.at[core, z, mx, :, lanes_of(j)]
        return dcopy(ref, ref, j, 12 + k, dev(dz=k))

    def agx(j, k, x):
        ref = sa.at[core, :, x, :, lanes_of(j)]
        return dcopy(ref, ref, j, 19 + k, dev(dx=k))

    def ags(j, k, b):
        ref = sa.at[b, :, ring_add(mx, -k, NX), :, lanes_of(j)]
        return dcopy(ref, ref, j, 23 + k, sib)

    def gathers(j, fn):
        if j < SPLITS:
            fn()
        else:
            pl.when(core == 1)(fn)

    def rsx_start(j):
        for k in range(1, NX):
            rsx(j, k).start()

    def rsx_done(j):
        for k in range(1, NX):
            rsx(j, k).wait_recv()
        total = t[j, :, 0, mx] + rx[j, 0]
        t[j, :, 0, mx] = total + (rx[j, 1] + rx[j, 2])
        for k in range(1, NZ):
            rsz(j, k).start()

    def rsz_done(j):
        for k in range(1, NZ):
            rsz(j, k).wait_recv()
        total = t[j, mz, 0, mx] + rz[j, 0]
        for k in range(1, NZ - 1, 2):
            total = total + (rz[j, k] + rz[j, k + 1])
        lanes = lanes_of(j)
        schur = kern[0:SHARE, lanes] - total
        own_s[0:SHARE, lanes] = schur

        def send():
            sa[core, mz, mx, :, lanes] = schur
            for k in range(1, NY):
                agy(j, k).start()
            for k in range(1, NZ):
                agz(j, k, mz).start()

        gathers(j, send)

    def agy_done(j):
        def go():
            agy(j, 1).wait_recv()
            for k in range(1, NZ):
                agz(j, k, mz).start()

        gathers(j, go)

    def agz_done(j):
        def go():
            for k in range(1, NZ):
                agz(j, k, ring_add(mz, -k, NZ)).wait_recv()
            for k in range(1, NX):
                agx(j, k, mx).start()
            ags(j, 0, core).start()

        gathers(j, go)

    def agx_done(j):
        def go():
            for k in range(1, NX):
                agx(j, k, ring_add(mx, -k, NX)).wait_recv()
                ags(j, k, core).start()

        gathers(j, go)

    def sib_done(j):
        def go():
            for k in range(NX):
                ags(j, k, 1 - core).wait_recv()

        if j < SPLITS:
            go()
        else:
            pl.when(core == 0)(go)

    def own_kernel():
        weights = wts[...]
        own_feat = feats[...].reshape(4 * SHARE, -1).astype(F32) * weights
        own_norm = jnp.sum(own_feat * own_feat, axis=1, keepdims=True)
        ids = lax.broadcasted_iota(jnp.int32, (4 * SHARE, BLOCK), 0)
        row_ids = ((ids // SHARE) * 8 + row) * BLOCK + col * SHARE + lax.rem(ids, SHARE)
        for b in range(PANELS):
            feat = fp[b].reshape(BLOCK, -1).astype(F32) * weights
            norm = nt(jnp.ones((8, feat.shape[1]), F32), feat * feat)[0:1, :]
            dist = own_norm + norm - 2.0 * nt(own_feat, feat)
            cols = lax.broadcasted_iota(jnp.int32, (4 * SHARE, BLOCK), 1) + b * BLOCK
            jitter = jnp.where(row_ids == cols, 0.01, 0.0).astype(F32)
            kern[:, b * BLOCK : (b + 1) * BLOCK] = jnp.exp(-0.5 * dist) + jitter

    @pl.when(at_y0)
    def _():
        fp[core, mz, mx] = feats[0]

    raw_copies[0].wait()
    pl.semaphore_wait(barrier, len(peers))

    @pl.when(at_y0)
    def _():
        for k in range(1, NY):
            f_y(k).start()
        f_z_start()
        for c in range(CHUNKS):
            relayout(0, c, [to_lf(0), to_pan])
            sib_chunk(c, core).start()
            ring_chunk(c).start()

    lo[...] = jnp.zeros(lo.shape, BF16)
    po[...] = jnp.zeros(po.shape, BF16)
    xs[7] = jnp.zeros((LANES, LANES), F32)
    dacc[...] = jnp.zeros((LANES, LANES), F32)
    col_buf[1] = jnp.zeros((n_cols, LANES), F32)
    sa[0, :, :, :, pl.ds(BLOCK, BLOCK)] = jnp.zeros((NZ, NX, SHARE, BLOCK), F32)
    for copy in raw_copies[1:]:
        copy.wait()

    def begin(b, hs, rnd):
        for h in hs:
            stream(b, h, rnd)[0]()

    @pl.when(at_y0)
    def _():
        for pair in range(2):
            for c in range(4 * pair, 4 * pair + 4):
                sib_chunk(c, 1 - core).wait_recv()
            product(0, pair, 0)
            rsx_start(2 * pair)
            rsx_start(2 * pair + 1)
        relayout_blocks(1)

        def rest(b):
            def go(i, carry):
                product(b, 0, i)
                product(b, 1, i)
                return carry

            lax.fori_loop(1, 4, go, 0)

        rest(0)
        begin(0, (0, 2), 1)
        f_x_start()
        product(1, 0, 0)
        product(1, 1, 0)
        for j in range(SPLITS):
            rsx_done(j)
        for j in range(SPLITS, 2 * SPLITS):
            rsx_start(j)
        rest(1)
        f_sib_start()
        begin(0, (1, 3), 1)
        begin(1, range(SPLITS), 1)
        f_sib(1 - core).wait_recv()
        own_kernel()
        for j in range(SPLITS):
            rsz_done(j)

    @pl.when(off_y0)
    def _():
        relayout_blocks(0)
        f_y(1).wait_recv()
        f_z_start()

        def whole(b, pair):
            def go(i, carry):
                product(b, pair, i)
                return carry

            lax.fori_loop(0, 4, go, 0)
            begin(b, (2 * pair, 2 * pair + 1), 0)

        for c in range(CHUNKS):
            ring_chunk(c).wait_recv()

            @pl.when(pos < NY - 1)
            def _():
                ring_chunk(c).start()

            sib_chunk(c, core).start()
            if c == 3:
                whole(core, 0)
                f_x_start()
        whole(core, 1)
        f_sib_start()
        for pair in range(2):
            for c in range(4 * pair, 4 * pair + 4):
                sib_chunk(c, 1 - core).wait_recv()
            whole(1 - core, pair)
        f_sib(1 - core).wait_recv()
        own_kernel()
        for j in range(SPLITS):
            agy_done(j)

    def store_inverse(b):
        def store(g, tile):
            xs[b, 8 * g : 8 * g + 8, :] = tile

        return store

    def block_of(value):
        return lambda v: value[8 * v : 8 * v + 8, :]

    def step(b):
        prev, after = lax.rem(b + 7, 8), lax.rem(b + 1, 8)
        here = pl.ds(pl.multiple_of(b * LANES, LANES), LANES)
        back = pl.ds(pl.multiple_of(prev * LANES, LANES), LANES)
        ahead = pl.ds(pl.multiple_of(after * LANES, LANES), LANES)
        last = col_buf.at[lax.rem(b + 1, 2)]
        corner = halves(nt(last[here, :], xs[prev]))
        block = sa[b // SPLITS, pl.ds(2 * lax.rem(b, SPLITS), 2), :, :, here]
        dg[...] = block.reshape(LANES, LANES) - dacc[...] - nt_halves(corner, corner)
        diag_inverse(block_of(dg[...]), store_inverse(b))
        for i, half in enumerate(halves(nt(last[...], xs[prev]))):
            lo[i, :, back] = half
        update = nt_halves((lo[0], lo[1]), (lo[0, here, :], lo[1, here, :]))
        col_buf[lax.rem(b, 2)] = sa[:, :, :, :, here].reshape(n_cols, LANES) - update
        below = (lo[0, ahead, :], lo[1, ahead, :])
        dacc[...] = nt_halves(below, below)

    def own_rows(b):
        lanes = pl.ds(pl.multiple_of(b * LANES, LANES), LANES)
        found = nt_halves((po[0], po[1]), (lo[0, lanes, :], lo[1, lanes, :]))
        panel = nt(own_s[:, lanes] - found, xs[b])
        out_ref[:, lanes] = panel
        for i, half in enumerate(halves(panel)):
            po[i, :, lanes] = half

    second = range(SPLITS, 2 * SPLITS)
    rs_hop(0, 0)
    agz_done(0)
    agz_done(1)
    agx_done(0)
    agz_done(2)
    agx_done(1)
    sib_done(0)

    def before_0():
        @pl.when(at_y0)
        def _():
            for j in second:
                rsx_done(j)

        rs_hop(1, 0)

    def before_1():
        agz_done(3)
        agx_done(2)
        sib_done(1)

        @pl.when(at_y0)
        def _():
            for j in second:
                rsz_done(j)

        rs_hop(0, 1)

    def before_2():
        agx_done(3)
        sib_done(2)

        @pl.when(off_y0)
        def _():
            for j in second:
                agy_done(j)

        rs_hop(2, 0)

    def before_3():
        sib_done(3)
        for j in second:
            agz_done(j)
        rs_hop(1, 1)

    def before_4():
        for j in second:
            agx_done(j)
        sib_done(4)
        rs_hop(3, 0)
        rs_hop(2, 1)

    def before_5():
        sib_done(5)
        rs_hop(4, 0)
        rs_hop(3, 1)

    def before_6():
        sib_done(6)
        rs_hop(5, 0)
        rs_hop(4, 1)

    def round_of(b, carry):
        before = (before_0, before_1, before_2, before_3, before_4, before_5, before_6)
        for k, fn in enumerate(before):
            pl.when(b == k)(fn)
        step(b)
        return carry

    lax.fori_loop(0, 7, round_of, 0)
    sib_done(7)
    rs_hop(5, 1)

    def own_schur(i):
        for q in range(PANELS * SPLITS):
            lanes = lanes_of(q)
            own_s[i * SHARE : (i + 1) * SHARE, lanes] = kern[i * SHARE : (i + 1) * SHARE, lanes] - t[q, mz, i, mx]

    pl.when(off_y0)(lambda: own_schur(0))
    for i in range(1, 4):
        own_schur(i)
    step(7)
    for b in range(8):
        own_rows(b)

    @pl.when(pos < NY - 1)
    def _():
        for c in range(CHUNKS):
            ring_chunk(c).wait_send()

    for c in range(CHUNKS):
        sib_chunk(c, core).wait_send()

    @pl.when(at_y0)
    def _():
        for k in range(1, NY):
            f_y(k).wait_send()

    for k in range(1, NZ):
        f_z(k, mz).wait_send()
    for k in range(1, NX):
        f_x(k, mx).wait_send()
    f_sib(core).wait_send()

    def drain_streams(rnd):
        for b in range(PANELS):
            for h in range(SPLITS):
                stream(b, h, rnd)[2]()

    pl.when(off_y0)(lambda: drain_streams(0))
    pl.when(at_y0)(lambda: drain_streams(1))
    for j in range(2 * SPLITS):
        @pl.when(at_y0)
        def _():
            for k in range(1, NX):
                rsx(j, k).wait_send()
            for k in range(1, NZ):
                rsz(j, k).wait_send()

            def sent():
                for k in range(1, NY):
                    agy(j, k).wait_send()

            gathers(j, sent)

        def sent_all():
            for k in range(1, NZ):
                agz(j, k, mz).wait_send()
            for k in range(1, NX):
                agx(j, k, mx).wait_send()
            for k in range(NX):
                ags(j, k, core).wait_send()

        gathers(j, sent_all)


def panels_of(lf, feats, wts):
    vmem = pl.BlockSpec(memory_space=pltpu.VMEM)
    anyspace = pl.BlockSpec(memory_space=pl.ANY)
    width = lf.shape[2] * lf.shape[3]
    fwidth = feats.shape[2]
    own, n = 4 * SHARE, PANELS * BLOCK
    dma = pltpu.SemaphoreType.DMA
    return pl.pallas_call(
        panels_kernel,
        out_shape=jax.ShapeDtypeStruct((own, n), F32),
        in_specs=[anyspace, vmem, vmem],
        out_specs=vmem,
        scratch_shapes=[
            pltpu.VMEM(lf.shape, BF16),
            pltpu.VMEM((SPLITS, 2 * CHUNK_ROWS, LANES), F32),
            pltpu.VMEM((4, BLOCK, width), BF16),
            pltpu.VMEM((PANELS, BLOCK, width), BF16),
            pltpu.VMEM((PANELS, NZ, NX, SHARE, fwidth), BF16),
            pltpu.VMEM((PANELS * SPLITS, NZ, 4, NX, SHARE, LANES), F32),
            pltpu.VMEM((own, n), F32),
            pltpu.VMEM((PANELS, 2, NZ - 1, 4, NX, SHARE, LANES), F32),
            pltpu.VMEM((PANELS, 2, NX - 1, NZ, 4, SHARE, LANES), F32),
            pltpu.VMEM((PANELS, 2, NX - 1, 4, SHARE, LANES), F32),
            pltpu.VMEM((PANELS, 2, NZ - 1, 4, SHARE, LANES), F32),
            pltpu.VMEM((PANELS * SPLITS, NX - 1, NZ, SHARE, LANES), F32),
            pltpu.VMEM((PANELS * SPLITS, NZ - 1, SHARE, LANES), F32),
            pltpu.VMEM((PANELS, NZ, NX, SHARE, n), F32),
            pltpu.VMEM((own, n), F32),
            pltpu.VMEM((2, n, n), BF16),
            pltpu.VMEM((n // LANES, LANES, LANES), F32),
            pltpu.VMEM((2, n, LANES), F32),
            pltpu.VMEM((LANES, LANES), F32),
            pltpu.VMEM((LANES, LANES), F32),
            pltpu.VMEM((2, own, n), BF16),
            dma((2, CHUNKS)), dma((2, CHUNKS)),
            dma((14,)), dma((14,)),
            dma((PANELS * SPLITS, 10)), dma((PANELS * SPLITS, 10)),
            dma((PANELS * SPLITS, 27)), dma((PANELS * SPLITS, 27)),
            dma((4,)),
        ],
        compiler_params=pltpu.CompilerParams(
            collective_id=0, has_side_effects=True, vmem_limit_bytes=58 * 2**20
        ),
    )(lf, feats, wts)


def per_device(features, left_factor, ard_weights):
    lf = left_factor.reshape(4, BLOCK, 2, -1)
    feats = features.reshape(4, SHARE, -1)
    panels = panels_of(lf, feats, ard_weights.reshape(1, -1))
    return panels.reshape(4, 1, 1, SHARE, PANELS * BLOCK)


def solution(mesh):
    return jax.shard_map(
        per_device,
        mesh=mesh,
        in_specs=(P(None, "row", "col", None, None), P(None, "row", None, None, "col", None), P()),
        out_specs=P(None, "row", "col", None, None),
        check_vma=False,
    )
```
